256 devices in a mesh: chan: 32 (over y, x, core), facet: 4 (over z_lo), vis: 2 (over z_hi).
Axes of the slice: x: 4, y: 4, z: 8 (z_hi: 2, z_lo: 4; z = z_hi * 4 + z_lo), core: 2. Of those that a mesh axis runs over, the one named last changes fastest.
Arguments:
- cube: float32 [32, 2048, 2048], P('chan', 'facet', 'vis'), may hold values from 0 to 1
- lowrank_dual: float32 [32, 2048, 2048], P('chan', 'facet', 'vis'), may hold values from -4 to 4
- vis_dual: float32 [32, 4, 2, 128, 128], P('chan', 'vis', None, 'facet'), may hold values from -3 to 3
- visibilities: float32 [32, 4, 2, 128, 128], P('chan', 'vis', None, 'facet'), may hold values from -3 to 3
- radii: float32 [32, 4], P('chan', 'vis'), may hold values from 32 to 128
- tiles: int32 [32, 4, 2], P('chan'), may hold values from 1 to 15
- facet_radius: float32 [4], P('facet'), may hold values from 512 to 4096
Outputs:
- cube_next: float32 [32, 2048, 2048], P('chan', 'facet', 'vis')
- lowrank_next: float32 [32, 2048, 2048], P('chan', 'facet', 'vis')
- vis_next: float32 [32, 4, 2, 128, 128], P('chan', 'vis', None, 'facet')
The draws below stay inside these ranges and needn't reach their ends.
Inputs may be any that keep to these rules, and one draw needn't show every extreme that they name: `tiles`: row and column tile indices of blocks of 128 by 128 grid cells; blocks may repeat.
All inputs are finite; a program needn't handle non-finite values.
Results may differ from the reference program's by a relative error of at most 0.0003.
Values sent between devices are 32-bit elements; how exact they have to be, the bound alone decides.
A program may use at most 128 MiB of HBM per device.

```python
import math
import jax
import jax.numpy as jnp
from jax import lax

IMAGE = 2048
TILE = 128
BLOCKS = 4
NS_STEPS = 10
ITERS = 2
CHANNELS = 32
FACETS = 4


def plant(values, key, least, top_value):
    longest = values.shape.index(max(values.shape))
    spots = []
    for shift in (0, 1):
        where = [jax.random.randint(jax.random.fold_in(key, axis), (), 0, length) for axis, length in enumerate(values.shape)]
        where[longest] = (where[longest] + shift) % values.shape[longest]
        spots.append(tuple(where))
    return values.at[spots[0]].set(least).at[spots[1]].set(top_value)


def levels(stream_key, extent, split, low, largest):
    loudness, own = 1.0, jax.random.fold_in(stream_key, 6)
    for dim, blocks in split:
        steps = jnp.exp(jax.random.uniform(jax.random.fold_in(own, dim), (blocks,), jnp.float32, low / len(split), largest / len(split)))
        loudness = loudness * jnp.repeat(steps, extent[dim] // blocks).reshape([-1 if axis == dim else 1 for axis in range(len(extent))])
    return loudness


def normal_values(key, extent, scale, bound, cuts=(), kind=jnp.bfloat16):
    gain = levels(key, extent, cuts, -0.22, 0.18) if cuts else 1.0
    result = jax.random.normal(key, extent, jnp.float32) * scale * gain
    return jnp.minimum(jnp.maximum(result, -bound), bound).astype(kind)


def setup_inputs(seed: int = 0) -> dict:
    seeds = jax.random.split(jax.random.key(seed), 8)
    return {
        "cube": jnp.clip(1.0 * jax.random.uniform(seeds[0], (CHANNELS, IMAGE, IMAGE), jnp.float32) ** levels(seeds[0], (CHANNELS, IMAGE, IMAGE), ((0, 32), (1, 4), (2, 2)), -0.2, 0.2), 0.0, 1.0),
        "lowrank_dual": normal_values(seeds[1], (CHANNELS, IMAGE, IMAGE), 0.5, 4.0, ((0, 32), (1, 4), (2, 2)), jnp.float32),
        "vis_dual": normal_values(seeds[2], (CHANNELS, BLOCKS, 2, TILE, TILE), 0.3, 3.0, ((0, 32), (1, 2), (3, 4)), jnp.float32),
        "visibilities": normal_values(seeds[3], (CHANNELS, BLOCKS, 2, TILE, TILE), 0.3, 3.0, ((0, 32), (1, 2), (3, 4)), jnp.float32),
        "radii": jnp.clip(jnp.exp(math.log(128.0) - 1.3862944 * jax.random.uniform(seeds[4], (CHANNELS, BLOCKS), jnp.float32) ** levels(seeds[4], (CHANNELS, BLOCKS), ((0, 32), (1, 2)), -0.2, 0.2)), 32.0, 128.0),
        "tiles": plant(jax.random.randint(seeds[5], (CHANNELS, BLOCKS, 2), 1, IMAGE // TILE), jax.random.fold_in(seeds[5], 1), 1, (IMAGE // TILE) - 1).astype(jnp.int32),
        "facet_radius": jnp.clip(jnp.exp(math.log(4096.0) - 2.0794415 * jax.random.uniform(seeds[6], (FACETS,), jnp.float32) ** levels(seeds[6], (FACETS,), ((0, 4),), -0.2, 0.2)), 512.0, 4096.0),
    }


step_size = 0.5
highest = lax.Precision.HIGHEST

def make_tables(index_rows, positions):
    angle = index_rows[..., None] * positions % IMAGE
    theta = angle.astype(jnp.float32) * (2.0 * math.pi / IMAGE)
    scale = 1.0 / math.sqrt(IMAGE)
    return (jnp.cos(theta) * scale, jnp.sin(theta) * scale)

def block_tables(tile_index, rows, cols):
    offsets = jnp.arange(TILE, dtype=jnp.int32)
    freq_rows = tile_index[:, 0:1] * TILE + offsets[None, :]
    freq_cols = tile_index[:, 1:2] * TILE + offsets[None, :]
    cos_u, sin_u = make_tables(freq_rows, rows)
    cos_v, sin_v = make_tables(freq_cols, cols)
    return (cos_u, sin_u, cos_v, sin_v)

def forward_blocks(image, cos_u, sin_u, cos_v, sin_v):
    wreal = jnp.einsum('pq,bvq->bpv', image, cos_v, precision=highest)
    wimag = -jnp.einsum('pq,bvq->bpv', image, sin_v, precision=highest)
    real = jnp.einsum('bup,bpv->buv', cos_u, wreal, precision=highest) + jnp.einsum('bup,bpv->buv', sin_u, wimag, precision=highest)
    imag = jnp.einsum('bup,bpv->buv', cos_u, wimag, precision=highest) - jnp.einsum('bup,bpv->buv', sin_u, wreal, precision=highest)
    return jnp.stack([real, imag], axis=1)

def adjoint_blocks(dual, cos_u, sin_u, cos_v, sin_v):
    dreal = dual[:, 0]
    dimag = dual[:, 1]
    ereal = jnp.einsum('bup,buv->bpv', cos_u, dreal, precision=highest) - jnp.einsum('bup,buv->bpv', sin_u, dimag, precision=highest)
    eimag = jnp.einsum('bup,buv->bpv', cos_u, dimag, precision=highest) + jnp.einsum('bup,buv->bpv', sin_u, dreal, precision=highest)
    return jnp.einsum('bpv,bvq->pq', ereal, cos_v, precision=highest) - jnp.einsum('bpv,bvq->pq', eimag, sin_v, precision=highest)

def inverse_root(gram, radius):
    count = gram.shape[0]
    eye = jnp.eye(count, dtype=jnp.float32)
    matrix = eye + gram / (radius * radius)
    trace = jnp.trace(matrix)
    current = matrix / trace
    inverse = eye
    for step in range(NS_STEPS):
        middle = 1.5 * eye - 0.5 * jnp.dot(inverse, current, precision=highest, preferred_element_type=jnp.float32)
        current = jnp.dot(current, middle, precision=highest, preferred_element_type=jnp.float32)
        inverse = jnp.dot(middle, inverse, precision=highest, preferred_element_type=jnp.float32)
    return inverse / jnp.sqrt(trace)

def reference(cube, lowrank_dual, vis_dual, visibilities, radii, tiles, facet_radius):
    positions = jnp.arange(IMAGE, dtype=jnp.int32)

    def forward_one(pair):
        image, tile_index = pair
        return forward_blocks(image, *block_tables(tile_index, positions, positions))

    def adjoint_one(pair):
        dual, tile_index = pair
        return adjoint_blocks(dual, *block_tables(tile_index, positions, positions))
    facet_rows = IMAGE // FACETS
    image_now = cube
    lowrank = lowrank_dual
    dual_now = vis_dual
    for step in range(ITERS):
        gradient = lax.map(adjoint_one, (dual_now, tiles))
        image_new = jnp.maximum(0.0, image_now - step_size * (lowrank + gradient))
        extrap = 2.0 * image_new - image_now
        summed = lowrank + extrap
        pieces = []
        for facet_index in range(FACETS):
            region = summed[:, facet_index * facet_rows:(facet_index + 1) * facet_rows, :]
            gram = jnp.einsum('lpq,mpq->lm', region, region, precision=highest)
            root = inverse_root(gram, facet_radius[facet_index])
            pieces.append(jnp.einsum('lpq,lm->mpq', region, root, precision=highest))
        lowrank = jnp.concatenate(pieces, axis=1)
        measured = lax.map(forward_one, (extrap, tiles))
        updated = dual_now + measured
        error = updated - visibilities
        norms = jnp.sqrt(lax.optimization_barrier(jnp.sum(error * error, axis=(2, 3, 4))))
        factor = radii / jnp.maximum(norms, radii)
        dual_now = updated - (visibilities + error * factor[:, :, None, None, None])
        image_now = image_new
    return (image_now, lowrank, dual_now)
```

```python
import functools
import math

import jax
import jax.numpy as jnp
from jax import lax
from jax.experimental import pallas as pl
from jax.experimental.pallas import tpu as pltpu
from jax.sharding import PartitionSpec as P

IMAGE = 2048
TILE = 128
NS_STEPS = 10
ITERS = 2
CHANNELS = 32
PITCH = 136


step_size = 0.5
highest = lax.Precision.HIGHEST


def make_tables(index_rows, positions):
    angle = index_rows[..., None] * positions % IMAGE
    theta = angle.astype(jnp.float32) * (2.0 * math.pi / IMAGE)
    scale = 1.0 / math.sqrt(IMAGE)
    return (jnp.cos(theta) * scale, jnp.sin(theta) * scale)


def block_tables(tile_index, rows, cols):
    offsets = jnp.arange(TILE, dtype=jnp.int32)
    freq_rows = tile_index[:, 0:1] * TILE + offsets[None, :]
    freq_cols = tile_index[:, 1:2] * TILE + offsets[None, :]
    cos_u, sin_u = make_tables(freq_rows, rows)
    cos_v, sin_v = make_tables(freq_cols, cols)
    return (cos_u, sin_u, cos_v, sin_v)


def forward_blocks(image, cos_u, sin_u, cos_v, sin_v):
    wreal = jnp.einsum("pq,bvq->bpv", image, cos_v, precision=highest)
    wimag = -jnp.einsum("pq,bvq->bpv", image, sin_v, precision=highest)
    real = jnp.einsum("bup,bpv->buv", cos_u, wreal, precision=highest) + jnp.einsum(
        "bup,bpv->buv", sin_u, wimag, precision=highest
    )
    imag = jnp.einsum("bup,bpv->buv", cos_u, wimag, precision=highest) - jnp.einsum(
        "bup,bpv->buv", sin_u, wreal, precision=highest
    )
    return jnp.stack([real, imag], axis=1)


def adjoint_blocks(dual, cos_u, sin_u, cos_v, sin_v):
    dreal = dual[:, 0]
    dimag = dual[:, 1]
    ereal = jnp.einsum("bup,buv->bpv", cos_u, dreal, precision=highest) - jnp.einsum(
        "bup,buv->bpv", sin_u, dimag, precision=highest
    )
    eimag = jnp.einsum("bup,buv->bpv", cos_u, dimag, precision=highest) + jnp.einsum(
        "bup,buv->bpv", sin_u, dreal, precision=highest
    )
    return jnp.einsum("bpv,bvq->pq", ereal, cos_v, precision=highest) - jnp.einsum(
        "bpv,bvq->pq", eimag, sin_v, precision=highest
    )


def chan_peer(offset):
    me = lax.axis_index("chan")
    dy, dx, dc = offset
    y = lax.rem(me // 8 + dy, 4)
    x = lax.rem(me // 2 + dx, 4)
    return (y * 4 + x) * 2 + lax.rem(me + dc, 2)


def hops(offset):
    return min(offset[0], 4 - offset[0]) + min(offset[1], 4 - offset[1])


OFFSETS = sorted(
    [(dy, dx, dc) for dy in range(4) for dx in range(4) for dc in range(2) if (dy, dx, dc) != (0, 0, 0)],
    key=lambda offset: -hops(offset),
)
GROUP_A = [(0, dx, dc) for dx in (2, 1, 3, 0) for dc in range(2) if (dx, dc) != (0, 0)]
GROUP_B = [(dy, dv) for dv in (1, 0) for dy in (2, 1, 3, 0) if (dy, dv) != (0, 0)]


def group_b_device(offset):
    me = lax.axis_index("chan")
    return {
        "chan": lax.rem(me // 8 + offset[0], 4) * 8 + lax.rem(me, 8),
        "vis": lax.rem(lax.axis_index("vis") + offset[1], 2),
    }


def remote(source, target, send_sem, recv_sem, device):
    return pltpu.make_async_remote_copy(
        src_ref=source,
        dst_ref=target,
        send_sem=send_sem,
        recv_sem=recv_sem,
        device_id=device,
        device_id_type=pl.DeviceIdType.MESH,
    )


def split_bf16(value):
    high = value.astype(jnp.bfloat16)
    return high, (value - high.astype(jnp.float32)).astype(jnp.bfloat16)


def entry_barrier():
    barrier = pltpu.get_barrier_semaphore()
    peers = [{"chan": chan_peer(offset)} for offset in OFFSETS]
    peers += [group_b_device(offset) for offset in GROUP_B if offset[1]]
    for device in peers:
        pl.semaphore_signal(barrier, inc=1, device_id=device, device_id_type=pl.DeviceIdType.MESH)
    pl.semaphore_wait(barrier, len(peers))


def exchange(source, target, sends, recvs):
    copies = []
    for n, offset in enumerate(OFFSETS):
        j = chan_peer(offset)
        copies.append(remote(source(j), target, sends.at[n], recvs.at[n], {"chan": j}))
        copies[-1].start()
    return copies


def sum_group(value, send_buf, recv_buf, sends, recvs, devices):
    send_buf[...] = value
    copies = []
    for n, device in enumerate(devices):
        copies.append(remote(send_buf, recv_buf.at[n], sends.at[n], recvs.at[n], device))
        copies[-1].start()
    for copy in copies:
        copy.wait()
    for n in range(len(devices)):
        value = value + recv_buf[n]
    return value


def stripes(group):
    return [pl.ds(group * 8 + s, CHANNELS, stride=PITCH) for s in range(8)]


def gram_of(received, halves):
    def body(group, total):
        block = jnp.concatenate([received[rows, :] for rows in stripes(group)], axis=1)
        both = jnp.concatenate(split_bf16(block), axis=0)
        halves[group] = both
        return total + lax.dot_general(
            both, both, (((1,), (1,)), ((), ())), preferred_element_type=jnp.float32
        )

    total = lax.fori_loop(0, TILE // 8, body, jnp.zeros((2 * CHANNELS, 2 * CHANNELS), jnp.float32))
    total = total[:CHANNELS] + total[CHANNELS:]
    return total[:, :CHANNELS] + total[:, CHANNELS:]


def mix_into(target, halves, root):
    high, low = split_bf16(root)
    weights = jnp.concatenate(
        [jnp.concatenate([high, high], axis=1), jnp.concatenate([low, low], axis=1)], axis=0
    )

    def body(group, carry):
        mixed = jnp.dot(weights, halves[group], preferred_element_type=jnp.float32)
        mixed = mixed[:CHANNELS] + mixed[CHANNELS:]
        for s, rows in enumerate(stripes(group)):
            target[rows, :] = mixed[:, s * 128 : (s + 1) * 128]
        return carry

    lax.fori_loop(0, TILE // 8, body, 0)


def matmul(a, b):
    return jnp.dot(a, b, precision=highest, preferred_element_type=jnp.float32)


def inverse_root(gram, radius):
    rows = lax.broadcasted_iota(jnp.int32, gram.shape, 0)
    eye = jnp.where(rows == lax.broadcasted_iota(jnp.int32, gram.shape, 1), 1.0, 0.0)
    matrix = eye + gram / (radius * radius)
    trace = jnp.sum(matrix * eye, axis=(0, 1), keepdims=True)
    current = matrix / trace
    inverse = eye
    for step in range(NS_STEPS):
        product = matmul(inverse, current) if step else current
        middle = 1.5 * eye - 0.5 * product
        inverse = matmul(middle, inverse) if step else middle
        if step < NS_STEPS - 1:
            current = matmul(current, middle)
    return inverse / jnp.sqrt(trace)


def pack(gram):
    return jnp.concatenate([gram[8 * k : 8 * k + 8] for k in range(4)], axis=1)


def unpack(packed):
    return jnp.concatenate([packed[:, 32 * k : 32 * k + 32] for k in range(4)], axis=0)


def lane_rows(index):
    return pl.ds(pl.multiple_of(index * PITCH, 8), TILE)


def lowrank_kernel(z_ref, radius_ref, p_ref, received, mixed, halves, sums, parts, sends, recvs, small_sends, small_recvs):
    me = lax.axis_index("chan")
    entry_barrier()
    received[lane_rows(me), :] = z_ref[me]
    copies = exchange(lambda j: z_ref.at[j], received.at[lane_rows(me), :], sends.at[0], recvs.at[0])
    for copy in copies:
        copy.wait()
    total = pack(gram_of(received, halves))
    total = sum_group(
        total, sums.at[0], parts.at[0], small_sends.at[0], small_recvs.at[0],
        [{"chan": chan_peer(offset)} for offset in GROUP_A],
    )
    total = sum_group(
        total, sums.at[1], parts.at[1], small_sends.at[1], small_recvs.at[1],
        [group_b_device(offset) for offset in GROUP_B],
    )
    root = inverse_root(unpack(total), radius_ref[0])
    mix_into(mixed, halves, root)
    p_ref[me] = mixed[lane_rows(me), :]
    copies = exchange(lambda j: mixed.at[lane_rows(j), :], p_ref.at[me], sends.at[1], recvs.at[1])
    for copy in copies:
        copy.wait()


def lowrank_step(tiles, radius, number):
    dma = pltpu.SemaphoreType.DMA
    return pl.pallas_call(
        lowrank_kernel,
        out_shape=jax.ShapeDtypeStruct((CHANNELS, TILE, TILE), jnp.float32),
        in_specs=[pl.BlockSpec(memory_space=pltpu.VMEM), pl.BlockSpec(memory_space=pltpu.SMEM)],
        out_specs=pl.BlockSpec(memory_space=pltpu.VMEM),
        scratch_shapes=[
            pltpu.VMEM((CHANNELS * PITCH, TILE), jnp.float32),
            pltpu.VMEM((CHANNELS * PITCH, TILE), jnp.float32),
            pltpu.VMEM((TILE // 8, 2 * CHANNELS, 1024), jnp.bfloat16),
            pltpu.VMEM((2, 8, 128), jnp.float32),
            pltpu.VMEM((2, 7, 8, 128), jnp.float32),
            dma((2, 31)),
            dma((2, 31)),
            dma((2, 7)),
            dma((2, 7)),
        ],
        compiler_params=pltpu.CompilerParams(
            collective_id=number, has_side_effects=True, vmem_limit_bytes=40 << 20
        ),
        name="lowrank",
    )(tiles, radius)


def on_device(cube, lowrank_dual, vis_dual, visibilities, radii, tiles, facet_radius):
    row_count = cube.shape[1]
    col_count = cube.shape[2]
    half_blocks = vis_dual.shape[1]
    quarter_rows = vis_dual.shape[3]
    facet_index = lax.axis_index("facet")
    column_index = lax.axis_index("vis")
    rows = facet_index * row_count + jnp.arange(row_count, dtype=jnp.int32)
    cols = column_index * col_count + jnp.arange(col_count, dtype=jnp.int32)
    tables = block_tables(tiles[0], rows, cols)
    image_now = cube[0]
    lowrank = lowrank_dual
    dual_now = vis_dual[0]
    for step in range(ITERS):
        dual_rows = lax.all_gather(dual_now, "facet", axis=2, tiled=True)
        dual_full = lax.all_gather(dual_rows, "vis", axis=0, tiled=True)
        gradient = adjoint_blocks(dual_full, *tables)
        image_new = jnp.maximum(0.0, image_now - step_size * (lowrank[0] + gradient))
        extrap = 2.0 * image_new - image_now
        summed = lowrank + extrap[None]
        pieces = summed[0].reshape(4, TILE, 8, TILE).transpose(0, 2, 1, 3)
        pieces = lowrank_step(pieces.reshape(CHANNELS, TILE, TILE), facet_radius, 0)
        lowrank = pieces.reshape(4, 8, TILE, TILE).transpose(0, 2, 1, 3).reshape(summed.shape)
        partial_value = forward_blocks(extrap, *tables)
        total = lax.psum(partial_value, ("facet", "vis"))
        owned = lax.dynamic_slice(
            total,
            (column_index * half_blocks, 0, facet_index * quarter_rows, 0),
            (half_blocks, 2, quarter_rows, total.shape[3]),
        )
        updated = dual_now + owned
        error = updated - visibilities[0]
        squares = jnp.sum(error * error, axis=(1, 2, 3))
        norms = jnp.sqrt(lax.psum(squares, "facet"))
        factor = radii[0] / jnp.maximum(norms, radii[0])
        dual_now = updated - (visibilities[0] + error * factor[:, None, None, None])
        image_now = image_new
    return (image_now[None], lowrank, dual_now[None])


def solution(mesh):
    placed = (
        P("chan", "facet", "vis"),
        P("chan", "facet", "vis"),
        P("chan", "vis", None, "facet", None),
        P("chan", "vis", None, "facet", None),
        P("chan", "vis"),
        P("chan", None, None),
        P("facet"),
    )
    return jax.shard_map(
        on_device,
        mesh=mesh,
        in_specs=placed,
        out_specs=(
            P("chan", "facet", "vis"),
            P("chan", "facet", "vis"),
            P("chan", "vis", None, "facet", None),
        ),
        check_vma=False,
    )
```

```python
import functools
import math

import jax
import jax.numpy as jnp
import numpy as np
from jax import lax
from jax.experimental import pallas as pl
from jax.experimental.pallas import tpu as pltpu
from jax.sharding import PartitionSpec as P

IMAGE = 2048
TILE = 128
BLOCKS = 4
NS_STEPS = 10
ITERS = 2
CHANNELS = 32
ROWS = 512
COLS = 1024
CHUNK = 256
PITCH = 136


step_size = 0.5
highest = lax.Precision.HIGHEST


def chan_peer(offset):
    me = lax.axis_index("chan")
    dy, dx, dc = offset
    y = lax.rem(me // 8 + dy, 4)
    x = lax.rem(me // 2 + dx, 4)
    return (y * 4 + x) * 2 + lax.rem(me + dc, 2)


def hops(offset):
    return min(offset[0], 4 - offset[0]) + min(offset[1], 4 - offset[1])


OFFSETS = sorted(
    [(dy, dx, dc) for dy in range(4) for dx in range(4) for dc in range(2) if (dy, dx, dc) != (0, 0, 0)],
    key=lambda offset: -hops(offset),
)
GROUP_A = [(0, dx, dc) for dx in (2, 1, 3, 0) for dc in range(2) if (dx, dc) != (0, 0)]
GROUP_B = [(dy, dv) for dv in (1, 0) for dy in (2, 1, 3, 0) if (dy, dv) != (0, 0)]


Z_OFFSETS = (4, 3, 5, 2, 6, 1, 7)


def group_b_device(offset):
    me = lax.axis_index("chan")
    return {
        "chan": lax.rem(me // 8 + offset[0], 4) * 8 + lax.rem(me, 8),
        "vis": lax.rem(lax.axis_index("vis") + offset[1], 2),
    }


def remote(source, target, send_sem, recv_sem, device):
    return pltpu.make_async_remote_copy(
        src_ref=source,
        dst_ref=target,
        send_sem=send_sem,
        recv_sem=recv_sem,
        device_id=device,
        device_id_type=pl.DeviceIdType.MESH,
    )


def split_bf16(value):
    high = value.astype(jnp.bfloat16)
    return high, (value - high.astype(jnp.float32)).astype(jnp.bfloat16)


def z_device(offset):
    z = lax.rem(lax.axis_index("vis") * 4 + lax.axis_index("facet") + offset, 8)
    return {"facet": lax.rem(z, 4), "vis": z // 4}


def facet_device(offset):
    return {"facet": lax.rem(lax.axis_index("facet") + offset, 4)}


def entry_barrier():
    barrier = pltpu.get_barrier_semaphore()
    peers = [{"chan": chan_peer(offset)} for offset in OFFSETS]
    peers += [group_b_device(offset) for offset in GROUP_B if offset[0] and offset[1]]
    peers += [z_device(offset) for offset in Z_OFFSETS]
    for device in peers:
        pl.semaphore_signal(barrier, inc=1, device_id=device, device_id_type=pl.DeviceIdType.MESH)
    pl.semaphore_wait(barrier, len(peers))


def sum_group(value, send_buf, recv_buf, sends, recvs, devices):
    send_buf[...] = value
    copies = []
    for n, device in enumerate(devices):
        copies.append(remote(send_buf, recv_buf.at[n], sends.at[n], recvs.at[n], device))
        copies[-1].start()
    for copy in copies:
        copy.wait()
    for n in range(len(devices)):
        value = value + recv_buf[n]
    return value


def stripes(group):
    return [pl.ds(group * 8 + s, CHANNELS, stride=PITCH) for s in range(8)]


def gram_of(received, halves):
    def body(group, total):
        block = jnp.concatenate([received[rows, :] for rows in stripes(group)], axis=1)
        both = jnp.concatenate(split_bf16(block), axis=0)
        halves[group] = both
        return total + lax.dot_general(
            both, both, (((1,), (1,)), ((), ())), preferred_element_type=jnp.float32
        )

    total = lax.fori_loop(0, TILE // 8, body, jnp.zeros((2 * CHANNELS, 2 * CHANNELS), jnp.float32))
    total = total[:CHANNELS] + total[CHANNELS:]
    return total[:, :CHANNELS] + total[:, CHANNELS:]


def mix_into(target, halves, root):
    high, low = split_bf16(root)
    weights = jnp.concatenate(
        [jnp.concatenate([high, high], axis=1), jnp.concatenate([low, low], axis=1)], axis=0
    )

    def body(group, carry):
        mixed = jnp.dot(weights, halves[group], preferred_element_type=jnp.float32)
        mixed = mixed[:CHANNELS] + mixed[CHANNELS:]
        for s, rows in enumerate(stripes(group)):
            target[rows, :] = mixed[:, s * 128 : (s + 1) * 128]
        return carry

    lax.fori_loop(0, TILE // 8, body, 0)


def matmul(a, b):
    return jnp.dot(a, b, precision=highest, preferred_element_type=jnp.float32)


def inverse_root(gram, radius):
    rows = lax.broadcasted_iota(jnp.int32, gram.shape, 0)
    eye = jnp.where(rows == lax.broadcasted_iota(jnp.int32, gram.shape, 1), 1.0, 0.0)
    matrix = eye + gram / (radius * radius)
    trace = jnp.sum(matrix * eye, axis=(0, 1), keepdims=True)
    current = matrix / trace
    inverse = eye
    for step in range(NS_STEPS):
        product = matmul(inverse, current) if step else current
        middle = 1.5 * eye - 0.5 * product
        inverse = matmul(middle, inverse) if step else middle
        if step < NS_STEPS - 1:
            current = matmul(current, middle)
    return inverse / jnp.sqrt(trace)


def pack(gram):
    return jnp.concatenate([gram[8 * k : 8 * k + 8] for k in range(4)], axis=1)


def unpack(packed):
    return jnp.concatenate([packed[:, 32 * k : 32 * k + 32] for k in range(4)], axis=0)


def lane_rows(index):
    return pl.ds(pl.multiple_of(index * PITCH, 8), TILE)


def waves():
    frequency = np.arange(TILE)
    angle = np.outer(frequency, np.arange(IMAGE)) % IMAGE * (2.0 * math.pi / IMAGE)
    table = np.stack([np.cos(angle), np.sin(angle)]) / math.sqrt(IMAGE)
    turn = np.outer(np.arange(16), np.arange(128)) % 16 * (2.0 * math.pi / 16)
    turns = np.stack([np.cos(turn), np.sin(turn)], axis=1)
    lanes = np.broadcast_to(turns[:, :, None, :], (16, 2, 8, 128))
    subs = np.broadcast_to(turns[:, :, :16, None], (16, 2, 16, 128))
    return [
        np.ascontiguousarray(value, dtype=np.float32)
        for value in (table, table.transpose(0, 2, 1), lanes, subs)
    ]


def turned(cosine, sine, turn, group):
    shape = cosine.shape
    cosine = cosine.reshape(shape[0] // group, group, shape[1])
    sine = sine.reshape(cosine.shape)
    c = cosine * turn[0] - sine * turn[1]
    s = sine * turn[0] + cosine * turn[1]
    return c.reshape(shape), s.reshape(shape)


def put(high_ref, low_ref, where, value):
    high, low = split_bf16(value)
    high_ref[where] = high
    low_ref[where] = low


def dot3(ah, al, bh, bl):
    def dot(a, b):
        return jnp.dot(a, b, preferred_element_type=jnp.float32)

    return dot(ah, bh) + dot(al, bh) + dot(ah, bl)


def build_tables(tiles_ref, wave_q, wave_p, waves_q, waves_p, lanes, subs, tabs):
    adj_h, adj_l, fwd_h, fwd_l, row_h, row_l, rowt_h, rowt_l = tabs

    def body(b, carry):
        turn_u = tiles_ref[b, 0]
        turn_v = tiles_ref[b, 1]
        lane_v = (lanes[turn_v, 0], lanes[turn_v, 1])
        lane_u = (lanes[turn_u, 0], lanes[turn_u, 1])
        sub_v = (subs[turn_v, 0], subs[turn_v, 1])
        sub_u = (subs[turn_u, 0], subs[turn_u, 1])
        first = pl.ds(pl.multiple_of(b * 256, 256), 128)
        second = pl.ds(pl.multiple_of(b * 256 + 128, 128), 128)
        for k in range(COLS // TILE):
            cols = slice(k * TILE, (k + 1) * TILE)
            half = slice(k % 2 * TILE, (k % 2 + 1) * TILE)
            c, s = turned(wave_q[0, :, cols], wave_q[1, :, cols], lane_v, 8)
            put(adj_h, adj_l, (k // 2, first, half), c)
            put(adj_h, adj_l, (k // 2, second, half), -s)
            c, s = turned(waves_q[0, cols], waves_q[1, cols], sub_v, 16)
            put(fwd_h, fwd_l, (b, cols, slice(0, 128)), c)
            put(fwd_h, fwd_l, (b, cols, slice(128, 256)), -s)
        for k in range(ROWS // TILE):
            cols = slice(k * TILE, (k + 1) * TILE)
            c, s = turned(wave_p[0, :, cols], wave_p[1, :, cols], lane_u, 8)
            put(row_h, row_l, (b, slice(0, 128), cols), c)
            put(row_h, row_l, (b, slice(128, 256), cols), s)
            c, s = turned(waves_p[0, cols], waves_p[1, cols], sub_u, 16)
            put(rowt_h, rowt_l, (b, cols, slice(0, 128)), c)
            put(rowt_h, rowt_l, (b, cols, slice(128, 256)), s)
        return carry

    lax.fori_loop(0, BLOCKS, body, 0)


def spread_rows(duals, rowt_h, rowt_l, e_h, e_l):
    def body(b, carry):
        side, block = b // 2, b % 2
        real = jnp.concatenate([duals[4 * side + f, block, 0] for f in range(4)], axis=0)
        imag = jnp.concatenate([duals[4 * side + f, block, 1] for f in range(4)], axis=0)
        both = jnp.concatenate(
            [jnp.concatenate([real, imag], axis=1), jnp.concatenate([-imag, real], axis=1)], axis=0
        )
        spread = dot3(rowt_h[b], rowt_l[b], *split_bf16(both))
        put(e_h, e_l, (slice(None), pl.ds(pl.multiple_of(b * 256, 256), 256)), spread)
        return carry

    lax.fori_loop(0, BLOCKS, body, 0)


def measure(x_h, x_l, tabs, values):
    adj_h, adj_l, fwd_h, fwd_l, row_h, row_l, rowt_h, rowt_l = tabs

    def body(b, carry):
        columns = dot3(x_h[...], x_l[...], fwd_h[b], fwd_l[b])
        quads = dot3(row_h[b], row_l[b], *split_bf16(columns))
        values[b, 0] = quads[:128, :128] + quads[128:, 128:]
        values[b, 1] = quads[:128, 128:] - quads[128:, :128]
        return carry

    lax.fori_loop(0, BLOCKS, body, 0)


def tile_place(j):
    rows = pl.ds(pl.multiple_of(j // 8 * TILE, TILE), TILE)
    cols = pl.ds(pl.multiple_of(lax.rem(j, 8) * TILE, TILE), TILE)
    return rows, cols


def negated(offset):
    return (-offset[0] % 4, -offset[1] % 4, -offset[2] % 2)


def imaging_kernel(
    x_hbm, p_hbm, dual_ref, data_ref, radii_ref, tiles_ref, radius_ref, wave_hbm, wavet_hbm, lanes, subs,
    x_out, p_out, dual_out,
    x_now, p_now, y_next, z_tiles, p_tiles, received, mixed, halves, x_h, x_l, e_h, e_l,
    adj_h, adj_l, fwd_h, fwd_l, row_h, row_l, rowt_h, rowt_l,
    wave_q, wave_p, waves_q, waves_p,
    duals, dual_mid, values, pieces, norm_send, norm_recv, sums, parts,
    local_sems, sends, recvs, z_sends, z_recvs, norm_sends, norm_recvs, small_sends, small_recvs,
):
    tabs = (adj_h, adj_l, fwd_h, fwd_l, row_h, row_l, rowt_h, rowt_l)
    me = lax.axis_index("chan")
    facet = lax.axis_index("facet")
    vis = lax.axis_index("vis")
    place = vis * 4 + facet
    at_q = pl.ds(pl.multiple_of(vis * COLS, COLS), COLS)
    at_p = pl.ds(pl.multiple_of(facet * ROWS, ROWS), ROWS)
    loads = [
        pltpu.make_async_copy(source, target, local_sems.at[n])
        for n, (source, target) in enumerate(
            [
                (wave_hbm.at[:, :, at_q], wave_q),
                (wave_hbm.at[:, :, at_p], wave_p),
                (wavet_hbm.at[:, at_q, :], waves_q),
                (wavet_hbm.at[:, at_p, :], waves_p),
                (x_hbm, x_now),
                (p_hbm, p_now),
            ]
        )
    ]
    for copy in loads:
        copy.start()
    entry_barrier()

    def gather_start(source, step):
        copies = []
        for n, offset in enumerate(Z_OFFSETS):
            copies.append(
                remote(source, duals.at[step, place], z_sends.at[step, n], z_recvs.at[step, n], z_device(offset))
            )
            copies[-1].start()
        return copies

    def column_chunk(d):
        return lax.rem(lax.rem(me // 2, 4) + d, 4)

    def adjoint_chunk(chunk):
        return dot3(e_h[...], e_l[...], adj_h[chunk], adj_l[chunk])

    index_of = {offset: n for n, offset in enumerate(OFFSETS)}

    def send_tile(step, source, target, offset):
        n = index_of[offset]
        copy = remote(source, target, sends.at[step, n], recvs.at[step, n], {"chan": chan_peer(offset)})
        copy.start()
        return copy

    def measure_and_update(step, dual_now, dual_next):
        measure(x_h, x_l, tabs, values)
        copies = []
        for n, offset in enumerate(Z_OFFSETS):
            device = z_device(offset)
            blocks = pl.ds(device["vis"] * 2, 2)
            rows = pl.ds(pl.multiple_of(device["facet"] * 32, 32), 32)
            copies.append(
                remote(values.at[blocks, :, rows, :], pieces.at[step, n], z_sends.at[2 + step, n],
                       z_recvs.at[2 + step, n], device)
            )
            copies[-1].start()
        for copy in copies:
            copy.wait()
        own = values[pl.ds(vis * 2, 2), :, pl.ds(pl.multiple_of(facet * 32, 32), 32), :]
        for n in range(len(Z_OFFSETS)):
            own = own + pieces[step, n]
        updated = dual_now[...] + own
        error = updated - data_ref[...]
        squares = jnp.sum((error * error).reshape(2, 8, 8, 128), axis=1)
        norm_send[step] = squares
        copies = []
        for n in range(3):
            copies.append(
                remote(norm_send.at[step], norm_recv.at[step, n], norm_sends.at[step, n], norm_recvs.at[step, n],
                       facet_device(n + 1))
            )
            copies[-1].start()
        for copy in copies:
            copy.wait()
        for n in range(3):
            squares = squares + norm_recv[step, n]
        for b in range(2):
            norm = jnp.sqrt(jnp.sum(squares[b], axis=(0, 1), keepdims=True))
            radius = radii_ref[b]
            factor = radius / jnp.maximum(norm, radius)
            dual_next[b] = updated[b] - (data_ref[b] + error[b] * factor)

    def gram_root(step):
        total = pack(gram_of(received.at[step], halves))
        total = sum_group(
            total, sums.at[2 * step], parts.at[2 * step], small_sends.at[2 * step], small_recvs.at[2 * step],
            [{"chan": chan_peer(offset)} for offset in GROUP_A],
        )
        return sum_group(
            total, sums.at[2 * step + 1], parts.at[2 * step + 1], small_sends.at[2 * step + 1],
            small_recvs.at[2 * step + 1], [group_b_device(offset) for offset in GROUP_B],
        )

    gathers = gather_start(dual_ref, 0)
    duals[0, place] = dual_ref[...]
    for copy in loads[:4]:
        copy.wait()
    build_tables(tiles_ref, wave_q, wave_p, waves_q, waves_p, lanes, subs, tabs)
    for copy in loads[4:]:
        copy.wait()
    for copy in gathers:
        copy.wait()
    spread_rows(duals.at[0], rowt_h, rowt_l, e_h, e_l)

    outward = []
    for d in (2, 1, 3, 0):
        chunk = column_chunk(d)
        gradient = adjoint_chunk(chunk)
        cols = pl.ds(pl.multiple_of(chunk * CHUNK, CHUNK), CHUNK)
        x = x_now[:, cols]
        p = p_now[:, cols]
        x_new = jnp.maximum(0.0, x - step_size * (p + gradient))
        bar = 2.0 * x_new - x
        x_now[:, cols] = x_new
        put(x_h, x_l, (slice(None), cols), bar)
        z = p + bar
        for i in range(4):
            for k in range(2):
                z_tiles[i * 8 + chunk * 2 + k] = z[i * TILE : (i + 1) * TILE, k * TILE : (k + 1) * TILE]
        for dy in (2, 1, 3, 0):
            for dc in range(2):
                offset = (dy, d, dc)
                if offset == (0, 0, 0):
                    received[0, lane_rows(me), :] = z_tiles[me]
                else:
                    outward.append(
                        send_tile(0, z_tiles.at[chan_peer(offset)], received.at[0, lane_rows(me), :], offset)
                    )

    measure_and_update(0, dual_ref, dual_mid)
    for copy in outward:
        copy.wait()
    total = gram_root(0)
    duals[1, place] = dual_mid[...]
    gathers = gather_start(dual_mid, 1)
    mix_into(mixed, halves, inverse_root(unpack(total), radius_ref[0]))
    backward = [
        send_tile(1, mixed.at[lane_rows(chan_peer(offset)), :], p_tiles.at[me], offset) for offset in OFFSETS
    ]
    p_tiles[me] = mixed[lane_rows(me), :]
    for copy in gathers:
        copy.wait()
    spread_rows(duals.at[1], rowt_h, rowt_l, e_h, e_l)

    def next_gradient(chunk, carry):
        cols = pl.ds(pl.multiple_of(chunk * CHUNK, CHUNK), CHUNK)
        y_next[:, cols] = x_now[:, cols] - step_size * adjoint_chunk(chunk)
        return carry

    lax.fori_loop(0, COLS // CHUNK, next_gradient, 0)

    outward = []
    for n, offset in enumerate(OFFSETS + [(0, 0, 0)]):
        away = negated(offset)
        j = chan_peer(away)
        if n < len(OFFSETS):
            backward[n].wait_recv()
        rows, cols = tile_place(j)
        x = x_now[rows, cols]
        p = p_tiles[j]
        x_new = jnp.maximum(0.0, y_next[rows, cols] - step_size * p)
        bar = 2.0 * x_new - x
        x_now[rows, cols] = x_new
        put(x_h, x_l, (rows, cols), bar)
        z = p + bar
        if n < len(OFFSETS):
            z_tiles[j] = z
            outward.append(send_tile(2, z_tiles.at[j], received.at[1, lane_rows(me), :], away))
        else:
            received[1, lane_rows(me), :] = z
    x_store = pltpu.make_async_copy(x_now, x_out, local_sems.at[6])
    x_store.start()
    measure_and_update(1, dual_mid, dual_out)
    for copy in backward:
        copy.wait_send()
    for copy in outward:
        copy.wait()
    total = gram_root(1)
    mix_into(mixed, halves, inverse_root(unpack(total), radius_ref[0]))
    rows, cols = tile_place(me)
    p_store = pltpu.make_async_copy(mixed.at[lane_rows(me), :], p_out.at[rows, cols], local_sems.at[7])
    p_store.start()
    backward = [
        send_tile(3, mixed.at[lane_rows(chan_peer(offset)), :], p_out.at[rows, cols], offset)
        for offset in OFFSETS
    ]
    x_store.wait()
    p_store.wait()
    for copy in backward:
        copy.wait()


def on_device(cube, lowrank_dual, vis_dual, visibilities, radii, tiles, facet_radius):
    f32, bf16 = jnp.float32, jnp.bfloat16
    dma = pltpu.SemaphoreType.DMA
    vmem = pl.BlockSpec(memory_space=pltpu.VMEM)
    smem = pl.BlockSpec(memory_space=pltpu.SMEM)
    anywhere = pl.BlockSpec(memory_space=pl.ANY)
    own = vis_dual.shape[1:]
    image = (ROWS, COLS)
    cube_next, lowrank_next, vis_next = pl.pallas_call(
        imaging_kernel,
        out_shape=[
            jax.ShapeDtypeStruct(image, f32),
            jax.ShapeDtypeStruct(image, f32),
            jax.ShapeDtypeStruct(own, f32),
        ],
        in_specs=[anywhere, anywhere, vmem, vmem, smem, smem, smem, anywhere, anywhere, vmem, vmem],
        out_specs=[anywhere, anywhere, vmem],
        scratch_shapes=[
            pltpu.VMEM(image, f32),
            pltpu.VMEM(image, f32),
            pltpu.VMEM(image, f32),
            pltpu.VMEM((CHANNELS, TILE, TILE), f32),
            pltpu.VMEM((CHANNELS, TILE, TILE), f32),
            pltpu.VMEM((2, CHANNELS * PITCH, TILE), f32),
            pltpu.VMEM((CHANNELS * PITCH, TILE), f32),
            pltpu.VMEM((TILE // 8, 2 * CHANNELS, 1024), bf16),
            pltpu.VMEM(image, bf16),
            pltpu.VMEM(image, bf16),
            pltpu.VMEM(image, bf16),
            pltpu.VMEM(image, bf16),
            pltpu.VMEM((COLS // CHUNK, BLOCKS * 256, CHUNK), bf16),
            pltpu.VMEM((COLS // CHUNK, BLOCKS * 256, CHUNK), bf16),
            pltpu.VMEM((BLOCKS, COLS, 256), bf16),
            pltpu.VMEM((BLOCKS, COLS, 256), bf16),
            pltpu.VMEM((BLOCKS, 256, ROWS), bf16),
            pltpu.VMEM((BLOCKS, 256, ROWS), bf16),
            pltpu.VMEM((BLOCKS, ROWS, 256), bf16),
            pltpu.VMEM((BLOCKS, ROWS, 256), bf16),
            pltpu.VMEM((2, TILE, COLS), f32),
            pltpu.VMEM((2, TILE, ROWS), f32),
            pltpu.VMEM((2, COLS, TILE), f32),
            pltpu.VMEM((2, ROWS, TILE), f32),
            pltpu.VMEM((2, 8) + own, f32),
            pltpu.VMEM(own, f32),
            pltpu.VMEM((BLOCKS, 2, TILE, TILE), f32),
            pltpu.VMEM((2, 7) + own, f32),
            pltpu.VMEM((2, 2, 8, 128), f32),
            pltpu.VMEM((2, 3, 2, 8, 128), f32),
            pltpu.VMEM((4, 8, 128), f32),
            pltpu.VMEM((4, 7, 8, 128), f32),
            dma((8,)),
            dma((4, 31)),
            dma((4, 31)),
            dma((4, 7)),
            dma((4, 7)),
            dma((2, 3)),
            dma((2, 3)),
            dma((4, 7)),
            dma((4, 7)),
        ],
        compiler_params=pltpu.CompilerParams(
            collective_id=0, has_side_effects=True, vmem_limit_bytes=56 << 20
        ),
        name="imaging",
    )(
        cube[0], lowrank_dual[0], vis_dual[0], visibilities[0], radii[0], tiles[0], facet_radius,
        *[jnp.asarray(value) for value in waves()],
    )
    return (cube_next[None], lowrank_next[None], vis_next[None])


def solution(mesh):
    placed = (
        P("chan", "facet", "vis"),
        P("chan", "facet", "vis"),
        P("chan", "vis", None, "facet", None),
        P("chan", "vis", None, "facet", None),
        P("chan", "vis"),
        P("chan", None, None),
        P("facet"),
    )
    return jax.shard_map(
        on_device,
        mesh=mesh,
        in_specs=placed,
        out_specs=(
            P("chan", "facet", "vis"),
            P("chan", "facet", "vis"),
            P("chan", "vis", None, "facet", None),
        ),
        check_vma=False,
    )
```

```python
import functools
import math

import jax
import jax.numpy as jnp
import numpy as np
from jax import lax
from jax.experimental import pallas as pl
from jax.experimental.pallas import tpu as pltpu
from jax.sharding import PartitionSpec as P

IMAGE = 2048
TILE = 128
BLOCKS = 4
NS_STEPS = 10
ITERS = 2
CHANNELS = 32
ROWS = 512
COLS = 1024
CHUNK = 256
PITCH = 136


step_size = 0.5
highest = lax.Precision.HIGHEST


def chan_peer(offset):
    me = lax.axis_index("chan")
    dy, dx, dc = offset
    y = lax.rem(me // 8 + dy, 4)
    x = lax.rem(me // 2 + dx, 4)
    return (y * 4 + x) * 2 + lax.rem(me + dc, 2)


OFFSETS = [
    (3, 3, 1), (2, 3, 0), (2, 2, 0), (1, 3, 1), (3, 1, 1), (3, 2, 1),
    (0, 1, 0), (2, 1, 1), (0, 1, 1), (0, 3, 1), (1, 1, 1), (3, 0, 1),
    (2, 2, 1), (2, 0, 0), (0, 2, 1), (3, 3, 0), (1, 2, 1), (1, 0, 0),
    (0, 0, 1), (0, 2, 0), (1, 0, 1), (2, 1, 0), (3, 0, 0), (2, 3, 1),
    (0, 3, 0), (3, 2, 0), (1, 2, 0), (1, 1, 0), (3, 1, 0), (1, 3, 0),
    (2, 0, 1),
]
GROUP_A = [(0, dx, dc) for dx in (2, 1, 3, 0) for dc in range(2) if (dx, dc) != (0, 0)]
GROUP_B = [(dy, dv) for dv in (1, 0) for dy in (2, 1, 3, 0) if (dy, dv) != (0, 0)]


Z_OFFSETS = (4, 3, 5, 2, 6, 1, 7)


def group_b_device(offset):
    me = lax.axis_index("chan")
    return {
        "chan": lax.rem(me // 8 + offset[0], 4) * 8 + lax.rem(me, 8),
        "vis": lax.rem(lax.axis_index("vis") + offset[1], 2),
    }


def remote(source, target, send_sem, recv_sem, device):
    return pltpu.make_async_remote_copy(
        src_ref=source,
        dst_ref=target,
        send_sem=send_sem,
        recv_sem=recv_sem,
        device_id=device,
        device_id_type=pl.DeviceIdType.MESH,
    )


def split_bf16(value):
    high = value.astype(jnp.bfloat16)
    return high, (value - high.astype(jnp.float32)).astype(jnp.bfloat16)


def z_device(offset):
    z = lax.rem(lax.axis_index("vis") * 4 + lax.axis_index("facet") + offset, 8)
    return {"facet": lax.rem(z, 4), "vis": z // 4}


def facet_device(offset):
    return {"facet": lax.rem(lax.axis_index("facet") + offset, 4)}


def entry_barrier():
    barrier = pltpu.get_barrier_semaphore()
    peers = [{"chan": chan_peer(offset)} for offset in OFFSETS]
    peers += [group_b_device(offset) for offset in GROUP_B if offset[0] and offset[1]]
    peers += [z_device(offset) for offset in Z_OFFSETS]
    for device in peers:
        pl.semaphore_signal(barrier, inc=1, device_id=device, device_id_type=pl.DeviceIdType.MESH)
    pl.semaphore_wait(barrier, len(peers))


def stripes(group):
    return [pl.ds(group * 8 + s, CHANNELS, stride=PITCH) for s in range(8)]


def gram_of(stripe, halves):
    def body(group, total):
        block = jnp.concatenate([stripe(rows) for rows in stripes(group)], axis=1)
        both = jnp.concatenate(split_bf16(block), axis=0)
        halves[group] = both
        return total + lax.dot_general(
            both, both, (((1,), (1,)), ((), ())), preferred_element_type=jnp.float32
        )

    total = lax.fori_loop(0, TILE // 8, body, jnp.zeros((2 * CHANNELS, 2 * CHANNELS), jnp.float32))
    total = total[:CHANNELS] + total[CHANNELS:]
    return total[:, :CHANNELS] + total[:, CHANNELS:]


def mix_into(target, halves, root):
    high, low = split_bf16(root)
    weights = jnp.concatenate(
        [jnp.concatenate([high, high], axis=1), jnp.concatenate([low, low], axis=1)], axis=0
    )

    def body(group, carry):
        mixed = jnp.dot(weights, halves[group], preferred_element_type=jnp.float32)
        mixed = mixed[:CHANNELS] + mixed[CHANNELS:]
        for s, rows in enumerate(stripes(group)):
            target[rows, :] = mixed[:, s * 128 : (s + 1) * 128]
        return carry

    lax.fori_loop(0, TILE // 8, body, 0)


def matmul(a, b):
    return jnp.dot(a, b, precision=highest, preferred_element_type=jnp.float32)


def inverse_root(gram, radius):
    rows = lax.broadcasted_iota(jnp.int32, gram.shape, 0)
    eye = jnp.where(rows == lax.broadcasted_iota(jnp.int32, gram.shape, 1), 1.0, 0.0)
    matrix = eye + gram / (radius * radius)
    trace = jnp.sum(matrix * eye, axis=(0, 1), keepdims=True)
    current = matrix / trace
    inverse = eye
    for step in range(NS_STEPS):
        product = matmul(inverse, current) if step else current
        middle = 1.5 * eye - 0.5 * product
        inverse = matmul(middle, inverse) if step else middle
        if step < NS_STEPS - 1:
            current = matmul(current, middle)
    return inverse / jnp.sqrt(trace)


def pack(gram):
    return jnp.concatenate([gram[8 * k : 8 * k + 8] for k in range(4)], axis=1)


def unpack(packed):
    return jnp.concatenate([packed[:, 32 * k : 32 * k + 32] for k in range(4)], axis=0)


def lane_rows(index):
    return pl.ds(pl.multiple_of(index * PITCH, 8), TILE)


def waves():
    frequency = np.arange(TILE)
    angle = np.outer(frequency, np.arange(IMAGE)) % IMAGE * (2.0 * math.pi / IMAGE)
    table = np.stack([np.cos(angle), np.sin(angle)]) / math.sqrt(IMAGE)
    turn = np.outer(np.arange(16), np.arange(128)) % 16 * (2.0 * math.pi / 16)
    turns = np.stack([np.cos(turn), np.sin(turn)], axis=1)
    lanes = np.broadcast_to(turns[:, :, None, :], (16, 2, 8, 128))
    subs = np.broadcast_to(turns[:, :, :16, None], (16, 2, 16, 128))
    return [
        np.ascontiguousarray(value, dtype=np.float32)
        for value in (table, table.transpose(0, 2, 1), lanes, subs)
    ]


def turned(cosine, sine, turn, group):
    shape = cosine.shape
    cosine = cosine.reshape(shape[0] // group, group, shape[1])
    sine = sine.reshape(cosine.shape)
    c = cosine * turn[0] - sine * turn[1]
    s = sine * turn[0] + cosine * turn[1]
    return c.reshape(shape), s.reshape(shape)


def put(high_ref, low_ref, where, value):
    high, low = split_bf16(value)
    high_ref[where] = high
    low_ref[where] = low


def dot3(ah, al, bh, bl):
    def dot(a, b):
        return jnp.dot(a, b, preferred_element_type=jnp.float32)

    return dot(ah, bh) + dot(al, bh) + dot(ah, bl)


def build_tables(tiles_ref, wave_q, wave_p, waves_q, waves_p, lanes, subs, tabs):
    adj_h, adj_l, fwd_h, fwd_l, row_h, row_l, rowt_h, rowt_l = tabs

    def body(b, carry):
        turn_u = tiles_ref[0, 0, b]
        turn_v = tiles_ref[0, 1, b]
        lane_v = (lanes[turn_v, 0], lanes[turn_v, 1])
        lane_u = (lanes[turn_u, 0], lanes[turn_u, 1])
        sub_v = (subs[turn_v, 0], subs[turn_v, 1])
        sub_u = (subs[turn_u, 0], subs[turn_u, 1])
        first = pl.ds(pl.multiple_of(b * 256, 256), 128)
        second = pl.ds(pl.multiple_of(b * 256 + 128, 128), 128)
        for k in range(COLS // TILE):
            cols = slice(k * TILE, (k + 1) * TILE)
            half = slice(k % 2 * TILE, (k % 2 + 1) * TILE)
            c, s = turned(wave_q[0, :, cols], wave_q[1, :, cols], lane_v, 8)
            put(adj_h, adj_l, (k // 2, first, half), c)
            put(adj_h, adj_l, (k // 2, second, half), -s)
            c, s = turned(waves_q[0, cols], waves_q[1, cols], sub_v, 16)
            put(fwd_h, fwd_l, (b, cols, slice(0, 128)), c)
            put(fwd_h, fwd_l, (b, cols, slice(128, 256)), -s)
        for k in range(ROWS // TILE):
            cols = slice(k * TILE, (k + 1) * TILE)
            c, s = turned(wave_p[0, :, cols], wave_p[1, :, cols], lane_u, 8)
            put(row_h, row_l, (b, slice(0, 128), cols), c)
            put(row_h, row_l, (b, slice(128, 256), cols), s)
            c, s = turned(waves_p[0, cols], waves_p[1, cols], sub_u, 16)
            put(rowt_h, rowt_l, (b, cols, slice(0, 128)), c)
            put(rowt_h, rowt_l, (b, cols, slice(128, 256)), s)
        return carry

    lax.fori_loop(0, BLOCKS, body, 0)


def spread_rows(duals, rowt_h, rowt_l, e_h, e_l):
    def body(b, carry):
        side, block = b // 2, b % 2
        real = jnp.concatenate([duals[4 * side + f, block, 0] for f in range(4)], axis=0)
        imag = jnp.concatenate([duals[4 * side + f, block, 1] for f in range(4)], axis=0)
        both = jnp.concatenate(
            [jnp.concatenate([real, imag], axis=1), jnp.concatenate([-imag, real], axis=1)], axis=0
        )
        spread = dot3(rowt_h[b], rowt_l[b], *split_bf16(both))
        put(e_h, e_l, (slice(None), pl.ds(pl.multiple_of(b * 256, 256), 256)), spread)
        return carry

    lax.fori_loop(0, BLOCKS, body, 0)


def measure(x_h, x_l, tabs, values):
    adj_h, adj_l, fwd_h, fwd_l, row_h, row_l, rowt_h, rowt_l = tabs

    def body(b, carry):
        columns = dot3(x_h[...], x_l[...], fwd_h[b], fwd_l[b])
        quads = dot3(row_h[b], row_l[b], *split_bf16(columns))
        values[b, 0] = quads[:128, :128] + quads[128:, 128:]
        values[b, 1] = quads[:128, 128:] - quads[128:, :128]
        return carry

    lax.fori_loop(0, BLOCKS, body, 0)


def tile_place(j):
    rows = pl.ds(pl.multiple_of(j // 8 * TILE, TILE), TILE)
    cols = pl.ds(pl.multiple_of(lax.rem(j, 8) * TILE, TILE), TILE)
    return rows, cols


def negated(offset):
    return (-offset[0] % 4, -offset[1] % 4, -offset[2] % 2)


def imaging_kernel(
    x_hbm, p_hbm, dual_ref, data_ref, radii_ref, tiles_ref, radius_ref, wave_hbm, wavet_hbm, lanes, subs,
    x_out, p_out, dual_out,
    x_now, p_now, change, slope, p_back, got_change, got_x, got_slope, mixed, halves, x_h, x_l, e_h, e_l,
    adj_h, adj_l, fwd_h, fwd_l, row_h, row_l, rowt_h, rowt_l,
    wave_q, wave_p, waves_q, waves_p,
    duals, dual_mid, values, pieces, norm_send, norm_recv, sums, parts,
    local_sems, sends, recvs, z_sends, z_recvs, norm_sends, norm_recvs, small_sends, small_recvs,
):
    tabs = (adj_h, adj_l, fwd_h, fwd_l, row_h, row_l, rowt_h, rowt_l)
    me = lax.axis_index("chan")
    facet = lax.axis_index("facet")
    vis = lax.axis_index("vis")
    place = vis * 4 + facet
    at_q = pl.ds(pl.multiple_of(vis * COLS, COLS), COLS)
    at_p = pl.ds(pl.multiple_of(facet * ROWS, ROWS), ROWS)
    loads = [
        pltpu.make_async_copy(source, target, local_sems.at[n])
        for n, (source, target) in enumerate(
            [
                (x_hbm, x_now),
                (p_hbm, p_now),
                (wave_hbm.at[:, :, at_q], wave_q),
                (wave_hbm.at[:, :, at_p], wave_p),
                (wavet_hbm.at[:, at_q, :], waves_q),
                (wavet_hbm.at[:, at_p, :], waves_p),
            ]
        )
    ]
    for copy in loads:
        copy.start()
    entry_barrier()

    def gather_start(source, step):
        copies = []
        for n, offset in enumerate(Z_OFFSETS):
            copies.append(
                remote(source, duals.at[step, place], z_sends.at[step, n], z_recvs.at[step, n], z_device(offset))
            )
            copies[-1].start()
        return copies

    def column_chunk(d):
        return lax.rem(lax.rem(me // 2, 4) + d, 4)

    def chunk_columns(chunk):
        return pl.ds(pl.multiple_of(chunk * CHUNK, CHUNK), CHUNK)

    def adjoint_chunk(chunk):
        return dot3(e_h[...], e_l[...], adj_h[chunk], adj_l[chunk])

    index_of = {offset: n for n, offset in enumerate(OFFSETS)}

    def send(step, source, target, offset):
        n = index_of[offset]
        copy = remote(source, target, sends.at[step, n], recvs.at[step, n], {"chan": chan_peer(offset)})
        copy.start()
        return copy

    def send_tiles(step, image, target, offsets):
        copies = []
        for offset in offsets:
            if offset == (0, 0, 0):
                target[lane_rows(me), :] = image[tile_place(me)]
            else:
                source = image.at[tile_place(chan_peer(offset))]
                copies.append(send(step, source, target.at[lane_rows(me), :], offset))
        return copies

    def send_back(step, target):
        return [send(step, mixed.at[step - 3, lane_rows(chan_peer(offset)), :], target, offset) for offset in OFFSETS]

    def scatter_start(step):
        measure(x_h, x_l, tabs, values)
        copies = []
        for n, offset in enumerate(Z_OFFSETS):
            device = z_device(offset)
            blocks = pl.ds(device["vis"] * 2, 2)
            rows = pl.ds(pl.multiple_of(device["facet"] * 32, 32), 32)
            copies.append(
                remote(values.at[blocks, :, rows, :], pieces.at[step, n], z_sends.at[2 + step, n],
                       z_recvs.at[2 + step, n], device)
            )
            copies[-1].start()
        return copies

    def update_dual(step, copies, dual_now, dual_next):
        for copy in copies:
            copy.wait()
        own = values[pl.ds(vis * 2, 2), :, pl.ds(pl.multiple_of(facet * 32, 32), 32), :]
        for n in range(len(Z_OFFSETS)):
            own = own + pieces[step, n]
        updated = dual_now[...] + own
        error = updated - data_ref[...]
        squares = jnp.sum((error * error).reshape(2, 8, 8, 128), axis=1)
        norm_send[step] = squares
        copies = []
        for n in range(3):
            copies.append(
                remote(norm_send.at[step], norm_recv.at[step, n], norm_sends.at[step, n], norm_recvs.at[step, n],
                       facet_device(n + 1))
            )
            copies[-1].start()
        for copy in copies:
            copy.wait()
        for n in range(3):
            squares = squares + norm_recv[step, n]
        for b in range(2):
            norm = jnp.sqrt(jnp.sum(squares[b], axis=(0, 1), keepdims=True))
            radius = radii_ref[0, b]
            factor = radius / jnp.maximum(norm, radius)
            dual_next[b] = updated[b] - (data_ref[b] + error[b] * factor)

    def sum_start(step, value, devices):
        sums[step] = value
        copies = []
        for n, device in enumerate(devices):
            copies.append(
                remote(sums.at[step], parts.at[step, n], small_sends.at[step, n], small_recvs.at[step, n], device)
            )
            copies[-1].start()
        return copies

    def sum_end(step, copies):
        for copy in copies:
            copy.wait()
        value = sums[step]
        for n in range(len(copies)):
            value = value + parts[step, n]
        return value

    group_a = [{"chan": chan_peer(offset)} for offset in GROUP_A]
    group_b = [group_b_device(offset) for offset in GROUP_B]

    gathers = gather_start(dual_ref, 0)
    duals[0, place] = dual_ref[...]
    for copy in loads[:2]:
        copy.wait()

    def subtract(k, carry):
        rows = pl.ds(pl.multiple_of(k * 64, 64), 64)
        change[rows, :] = p_now[rows, :] - x_now[rows, :]
        return carry

    lax.fori_loop(0, ROWS // 64, subtract, 0)
    first = send_tiles(0, change, got_change, OFFSETS + [(0, 0, 0)])
    for copy in loads[2:]:
        copy.wait()
    build_tables(tiles_ref, wave_q, wave_p, waves_q, waves_p, lanes, subs, tabs)
    for copy in gathers:
        copy.wait()
    spread_rows(duals.at[0], rowt_h, rowt_l, e_h, e_l)

    for d in (2, 1, 3, 0):
        chunk = column_chunk(d)
        cols = chunk_columns(chunk)
        x = x_now[:, cols]
        x_new = jnp.maximum(0.0, x - step_size * (p_now[:, cols] + adjoint_chunk(chunk)))
        put(x_h, x_l, (slice(None), cols), 2.0 * x_new - x)
        x_now[:, cols] = x_new
    first += send_tiles(1, x_now, got_x, OFFSETS + [(0, 0, 0)])

    update_dual(0, scatter_start(0), dual_ref, dual_mid)
    gathers = gather_start(dual_mid, 1)
    duals[1, place] = dual_mid[...]
    for copy in first:
        copy.wait()
    total = pack(gram_of(lambda rows: got_change[rows, :] + 2.0 * got_x[rows, :], halves))
    small = sum_start(0, total, group_a)
    for copy in gathers:
        copy.wait()
    spread_rows(duals.at[1], rowt_h, rowt_l, e_h, e_l)
    for d in (2, 1, 3, 0):
        chunk = column_chunk(d)
        slope[:, chunk_columns(chunk)] = adjoint_chunk(chunk)
        if d == 2:
            small = sum_start(1, sum_end(0, small), group_b)
    second = send_tiles(2, slope, got_slope, OFFSETS + [(0, 0, 0)])
    total = sum_end(1, small)
    mix_into(mixed.at[0], halves, inverse_root(unpack(total), radius_ref[0]))
    third = send_back(3, p_back.at[me])
    p_back[me] = mixed[0, lane_rows(me), :]
    for copy in second:
        copy.wait()
    total = gram_of(
        lambda rows: jnp.maximum(mixed[0, rows, :] - got_x[rows, :], got_x[rows, :] - got_slope[rows, :]), halves
    )
    total = sum_end(2, sum_start(2, pack(total), group_a))
    total = sum_end(3, sum_start(3, total, group_b))
    mix_into(mixed.at[1], halves, inverse_root(unpack(total), radius_ref[0]))
    rows, cols = tile_place(me)
    p_store = pltpu.make_async_copy(mixed.at[1, lane_rows(me), :], p_out.at[rows, cols], local_sems.at[7])
    p_store.start()
    fourth = send_back(4, p_out.at[rows, cols])

    for n, offset in enumerate(OFFSETS + [(0, 0, 0)]):
        j = chan_peer(negated(offset))
        if n < len(OFFSETS):
            third[n].wait_recv()
        rows, cols = tile_place(j)
        x = x_now[rows, cols]
        x_new = jnp.maximum(0.0, x - step_size * (p_back[j] + slope[rows, cols]))
        put(x_h, x_l, (rows, cols), 2.0 * x_new - x)
        x_now[rows, cols] = x_new
    x_store = pltpu.make_async_copy(x_now, x_out, local_sems.at[6])
    x_store.start()
    update_dual(1, scatter_start(1), dual_mid, dual_out)
    for copy in third:
        copy.wait_send()
    x_store.wait()
    p_store.wait()
    for copy in fourth:
        copy.wait()


def store_kernel(x_in, p_in, dual_in, x_out, p_out, dual_out, x_buf, p_buf, dual_buf, load_sems, store_sems):
    moves = []
    for source, buffer, target in ((x_in, x_buf, x_out), (p_in, p_buf, p_out)):
        for k in range(4):
            rows = slice(k * 128, (k + 1) * 128)
            moves.append((source.at[rows], buffer.at[rows], target.at[0, rows]))
    moves.append((dual_in, dual_buf, dual_out.at[0]))
    loads = [pltpu.make_async_copy(a, b, load_sems.at[n]) for n, (a, b, c) in enumerate(moves)]
    stores = [pltpu.make_async_copy(b, c, store_sems.at[n]) for n, (a, b, c) in enumerate(moves)]
    for copy in loads:
        copy.start()
    for load, store in zip(loads, stores):
        load.wait()
        store.start()
    for copy in stores:
        copy.wait()


def on_device(cube, lowrank_dual, vis_dual, visibilities, radii, tiles, facet_radius):
    f32, bf16 = jnp.float32, jnp.bfloat16
    dma = pltpu.SemaphoreType.DMA
    vmem = pl.BlockSpec(memory_space=pltpu.VMEM)
    smem = pl.BlockSpec(memory_space=pltpu.SMEM)
    anywhere = pl.BlockSpec(memory_space=pl.ANY)
    own = vis_dual.shape[1:]
    image = (ROWS, COLS)
    cube_next, lowrank_next, vis_next = pl.pallas_call(
        imaging_kernel,
        out_shape=[
            jax.ShapeDtypeStruct(image, f32),
            jax.ShapeDtypeStruct(image, f32),
            jax.ShapeDtypeStruct(own, f32),
        ],
        in_specs=[anywhere, anywhere, vmem, vmem, smem, smem, smem, anywhere, anywhere, vmem, vmem],
        out_specs=[anywhere, anywhere, vmem],
        scratch_shapes=[
            pltpu.VMEM(image, f32),
            pltpu.VMEM(image, f32),
            pltpu.VMEM(image, f32),
            pltpu.VMEM(image, f32),
            pltpu.VMEM((CHANNELS, TILE, TILE), f32),
            pltpu.VMEM((CHANNELS * PITCH, TILE), f32),
            pltpu.VMEM((CHANNELS * PITCH, TILE), f32),
            pltpu.VMEM((CHANNELS * PITCH, TILE), f32),
            pltpu.VMEM((2, CHANNELS * PITCH, TILE), f32),
            pltpu.VMEM((TILE // 8, 2 * CHANNELS, 1024), bf16),
            pltpu.VMEM(image, bf16),
            pltpu.VMEM(image, bf16),
            pltpu.VMEM(image, bf16),
            pltpu.VMEM(image, bf16),
            pltpu.VMEM((COLS // CHUNK, BLOCKS * 256, CHUNK), bf16),
            pltpu.VMEM((COLS // CHUNK, BLOCKS * 256, CHUNK), bf16),
            pltpu.VMEM((BLOCKS, COLS, 256), bf16),
            pltpu.VMEM((BLOCKS, COLS, 256), bf16),
            pltpu.VMEM((BLOCKS, 256, ROWS), bf16),
            pltpu.VMEM((BLOCKS, 256, ROWS), bf16),
            pltpu.VMEM((BLOCKS, ROWS, 256), bf16),
            pltpu.VMEM((BLOCKS, ROWS, 256), bf16),
            pltpu.VMEM((2, TILE, COLS), f32),
            pltpu.VMEM((2, TILE, ROWS), f32),
            pltpu.VMEM((2, COLS, TILE), f32),
            pltpu.VMEM((2, ROWS, TILE), f32),
            pltpu.VMEM((2, 8) + own, f32),
            pltpu.VMEM(own, f32),
            pltpu.VMEM((BLOCKS, 2, TILE, TILE), f32),
            pltpu.VMEM((2, 7) + own, f32),
            pltpu.VMEM((2, 2, 8, 128), f32),
            pltpu.VMEM((2, 3, 2, 8, 128), f32),
            pltpu.VMEM((4, 8, 128), f32),
            pltpu.VMEM((4, 7, 8, 128), f32),
            dma((8,)),
            dma((5, 31)),
            dma((5, 31)),
            dma((4, 7)),
            dma((4, 7)),
            dma((2, 3)),
            dma((2, 3)),
            dma((4, 7)),
            dma((4, 7)),
        ],
        compiler_params=pltpu.CompilerParams(
            collective_id=0, has_side_effects=True, vmem_limit_bytes=56 << 20
        ),
        name="imaging",
    )(
        cube[0], lowrank_dual[0], vis_dual[0], visibilities[0], radii, jnp.swapaxes(tiles, 1, 2), facet_radius,
        *[jnp.asarray(value) for value in waves()],
    )
    return pl.pallas_call(
        store_kernel,
        out_shape=[
            jax.ShapeDtypeStruct((1,) + image, f32),
            jax.ShapeDtypeStruct((1,) + image, f32),
            jax.ShapeDtypeStruct((1,) + own, f32),
        ],
        in_specs=[anywhere] * 3,
        out_specs=[anywhere] * 3,
        scratch_shapes=[pltpu.VMEM(image, f32), pltpu.VMEM(image, f32), pltpu.VMEM(own, f32), dma((9,)), dma((9,))],
        compiler_params=pltpu.CompilerParams(vmem_limit_bytes=56 << 20),
        name="store",
    )(cube_next, lowrank_next, vis_next)


def solution(mesh):
    placed = (
        P("chan", "facet", "vis"),
        P("chan", "facet", "vis"),
        P("chan", "vis", None, "facet", None),
        P("chan", "vis", None, "facet", None),
        P("chan", "vis"),
        P("chan", None, None),
        P("facet"),
    )
    return jax.shard_map(
        on_device,
        mesh=mesh,
        in_specs=placed,
        out_specs=(
            P("chan", "facet", "vis"),
            P("chan", "facet", "vis"),
            P("chan", "vis", None, "facet", None),
        ),
        check_vma=False,
    )
```

```python
import functools
import math

import jax
import jax.numpy as jnp
import numpy as np
from jax import lax
from jax.experimental import pallas as pl
from jax.experimental.pallas import tpu as pltpu
from jax.sharding import PartitionSpec as P

IMAGE = 2048
TILE = 128
BLOCKS = 4
NS_STEPS = 10
ITERS = 2
CHANNELS = 32
ROWS = 512
COLS = 1024
CHUNK = 256
PITCH = 136


step_size = 0.5
highest = lax.Precision.HIGHEST


def chan_peer(offset):
    me = lax.axis_index("chan")
    dy, dx, dc = offset
    y = lax.rem(me // 8 + dy, 4)
    x = lax.rem(me // 2 + dx, 4)
    return (y * 4 + x) * 2 + lax.rem(me + dc, 2)


OFFSETS = [
    (3, 3, 1), (2, 3, 0), (2, 2, 0), (1, 3, 1), (3, 1, 1), (3, 2, 1),
    (0, 1, 0), (2, 1, 1), (0, 1, 1), (0, 3, 1), (1, 1, 1), (3, 0, 1),
    (2, 2, 1), (2, 0, 0), (0, 2, 1), (3, 3, 0), (1, 2, 1), (1, 0, 0),
    (0, 0, 1), (0, 2, 0), (1, 0, 1), (2, 1, 0), (3, 0, 0), (2, 3, 1),
    (0, 3, 0), (3, 2, 0), (1, 2, 0), (1, 1, 0), (3, 1, 0), (1, 3, 0),
    (2, 0, 1),
]
GROUP_A = [(0, dx, dc) for dx in (2, 1, 3, 0) for dc in range(2) if (dx, dc) != (0, 0)]
GROUP_B = [(dy, dv) for dv in (1, 0) for dy in (2, 1, 3, 0) if (dy, dv) != (0, 0)]


Z_OFFSETS = (4, 3, 5, 2, 6, 1, 7)


def group_b_device(offset):
    me = lax.axis_index("chan")
    return {
        "chan": lax.rem(me // 8 + offset[0], 4) * 8 + lax.rem(me, 8),
        "vis": lax.rem(lax.axis_index("vis") + offset[1], 2),
    }


def remote(source, target, send_sem, recv_sem, device):
    return pltpu.make_async_remote_copy(
        src_ref=source,
        dst_ref=target,
        send_sem=send_sem,
        recv_sem=recv_sem,
        device_id=device,
        device_id_type=pl.DeviceIdType.MESH,
    )


def split_bf16(value):
    high = value.astype(jnp.bfloat16)
    return high, (value - high.astype(jnp.float32)).astype(jnp.bfloat16)


def z_device(offset):
    z = lax.rem(lax.axis_index("vis") * 4 + lax.axis_index("facet") + offset, 8)
    return {"facet": lax.rem(z, 4), "vis": z // 4}


def facet_device(offset):
    return {"facet": lax.rem(lax.axis_index("facet") + offset, 4)}


def entry_barrier():
    barrier = pltpu.get_barrier_semaphore()
    peers = [{"chan": chan_peer(offset)} for offset in OFFSETS]
    peers += [group_b_device(offset) for offset in GROUP_B if offset[0] and offset[1]]
    peers += [z_device(offset) for offset in Z_OFFSETS]
    for device in peers:
        pl.semaphore_signal(barrier, inc=1, device_id=device, device_id_type=pl.DeviceIdType.MESH)
    pl.semaphore_wait(barrier, len(peers))


def stripes(group):
    return [pl.ds(group * 8 + s, CHANNELS, stride=PITCH) for s in range(8)]


def gram_of(stripe, halves):
    def body(group, total):
        block = jnp.concatenate([stripe(rows) for rows in stripes(group)], axis=1)
        both = jnp.concatenate(split_bf16(block), axis=0)
        halves[group] = both
        return total + lax.dot_general(
            both, both, (((1,), (1,)), ((), ())), preferred_element_type=jnp.float32
        )

    total = lax.fori_loop(
        0, TILE // 8, body, jnp.zeros((2 * CHANNELS, 2 * CHANNELS), jnp.float32), unroll=4
    )
    total = total[:CHANNELS] + total[CHANNELS:]
    return total[:, :CHANNELS] + total[:, CHANNELS:]


def mix_into(target, halves, root):
    high, low = split_bf16(root)
    weights = jnp.concatenate(
        [jnp.concatenate([high, high], axis=1), jnp.concatenate([low, low], axis=1)], axis=0
    )

    def body(group, carry):
        mixed = jnp.dot(weights, halves[group], preferred_element_type=jnp.float32)
        mixed = mixed[:CHANNELS] + mixed[CHANNELS:]
        for s, rows in enumerate(stripes(group)):
            target[rows, :] = mixed[:, s * 128 : (s + 1) * 128]
        return carry

    lax.fori_loop(0, TILE // 8, body, 0, unroll=4)


def matmul(a, b):
    return jnp.dot(a, b, precision=highest, preferred_element_type=jnp.float32)


def inverse_root(gram, radius):
    rows = lax.broadcasted_iota(jnp.int32, gram.shape, 0)
    eye = jnp.where(rows == lax.broadcasted_iota(jnp.int32, gram.shape, 1), 1.0, 0.0)
    matrix = eye + gram / (radius * radius)
    trace = jnp.sum(matrix * eye, axis=(0, 1), keepdims=True)
    current = matrix / trace
    inverse = eye
    for step in range(NS_STEPS):
        product = matmul(inverse, current) if step else current
        middle = 1.5 * eye - 0.5 * product
        inverse = matmul(middle, inverse) if step else middle
        if step < NS_STEPS - 1:
            current = matmul(current, middle)
    return inverse / jnp.sqrt(trace)


def pack(gram):
    return jnp.concatenate([gram[8 * k : 8 * k + 8] for k in range(4)], axis=1)


def unpack(packed):
    return jnp.concatenate([packed[:, 32 * k : 32 * k + 32] for k in range(4)], axis=0)


def lane_rows(index):
    return pl.ds(pl.multiple_of(index * PITCH, 8), TILE)


def waves():
    frequency = np.arange(TILE)
    angle = np.outer(frequency, np.arange(IMAGE)) % IMAGE * (2.0 * math.pi / IMAGE)
    table = np.stack([np.cos(angle), np.sin(angle)]) / math.sqrt(IMAGE)
    turn = np.outer(np.arange(16), np.arange(128)) % 16 * (2.0 * math.pi / 16)
    turns = np.stack([np.cos(turn), np.sin(turn)], axis=1)
    lanes = np.broadcast_to(turns[:, :, None, :], (16, 2, 8, 128))
    subs = np.broadcast_to(turns[:, :, :16, None], (16, 2, 16, 128))
    return [
        np.ascontiguousarray(value, dtype=np.float32)
        for value in (table, table.transpose(0, 2, 1), lanes, subs)
    ]


def turned(cosine, sine, turn, group):
    shape = cosine.shape
    cosine = cosine.reshape(shape[0] // group, group, shape[1])
    sine = sine.reshape(cosine.shape)
    c = cosine * turn[0] - sine * turn[1]
    s = sine * turn[0] + cosine * turn[1]
    return c.reshape(shape), s.reshape(shape)


def put(high_ref, low_ref, where, value):
    high, low = split_bf16(value)
    high_ref[where] = high
    low_ref[where] = low


def dot3(ah, al, bh, bl):
    def dot(a, b):
        return jnp.dot(a, b, preferred_element_type=jnp.float32)

    return dot(ah, bh) + dot(al, bh) + dot(ah, bl)


def build_tables(tiles_ref, wave_q, wave_p, waves_q, waves_p, lanes, subs, tabs):
    adj_h, adj_l, fwd_h, fwd_l, row_h, row_l, rowt_h, rowt_l = tabs

    def body(b, carry):
        turn_u = tiles_ref[0, 0, b]
        turn_v = tiles_ref[0, 1, b]
        lane_v = (lanes[turn_v, 0], lanes[turn_v, 1])
        lane_u = (lanes[turn_u, 0], lanes[turn_u, 1])
        sub_v = (subs[turn_v, 0], subs[turn_v, 1])
        sub_u = (subs[turn_u, 0], subs[turn_u, 1])
        first = pl.ds(pl.multiple_of(b * 256, 256), 128)
        second = pl.ds(pl.multiple_of(b * 256 + 128, 128), 128)
        for k in range(COLS // TILE):
            cols = slice(k * TILE, (k + 1) * TILE)
            half = slice(k % 2 * TILE, (k % 2 + 1) * TILE)
            c, s = turned(wave_q[0, :, cols], wave_q[1, :, cols], lane_v, 8)
            put(adj_h, adj_l, (k // 2, first, half), c)
            put(adj_h, adj_l, (k // 2, second, half), -s)
            c, s = turned(waves_q[0, cols], waves_q[1, cols], sub_v, 16)
            put(fwd_h, fwd_l, (b, cols, slice(0, 128)), c)
            put(fwd_h, fwd_l, (b, cols, slice(128, 256)), -s)
        for k in range(ROWS // TILE):
            cols = slice(k * TILE, (k + 1) * TILE)
            c, s = turned(wave_p[0, :, cols], wave_p[1, :, cols], lane_u, 8)
            put(row_h, row_l, (b, slice(0, 128), cols), c)
            put(row_h, row_l, (b, slice(128, 256), cols), s)
            c, s = turned(waves_p[0, cols], waves_p[1, cols], sub_u, 16)
            put(rowt_h, rowt_l, (b, cols, slice(0, 128)), c)
            put(rowt_h, rowt_l, (b, cols, slice(128, 256)), s)
        return carry

    lax.fori_loop(0, BLOCKS, body, 0)


def spread_rows(duals, gain_of, rowt_h, rowt_l, e_h, e_l):
    def body(b, carry):
        side, block = b // 2, b % 2
        real = jnp.concatenate([duals[4 * side + f, block, 0] for f in range(4)], axis=0)
        imag = jnp.concatenate([duals[4 * side + f, block, 1] for f in range(4)], axis=0)
        if gain_of is not None:
            gain = gain_of(side, block, jnp.sum(real * real + imag * imag, axis=(0, 1), keepdims=True))
            real, imag = real * gain, imag * gain
        both = jnp.concatenate(
            [jnp.concatenate([real, imag], axis=1), jnp.concatenate([-imag, real], axis=1)], axis=0
        )
        spread = dot3(rowt_h[b], rowt_l[b], *split_bf16(both))
        put(e_h, e_l, (slice(None), pl.ds(pl.multiple_of(b * 256, 256), 256)), spread)
        return carry

    lax.fori_loop(0, BLOCKS, body, 0)


def measure(b, x_h, x_l, tabs, values):
    adj_h, adj_l, fwd_h, fwd_l, row_h, row_l, rowt_h, rowt_l = tabs
    columns = dot3(x_h[...], x_l[...], fwd_h[b], fwd_l[b])
    quads = dot3(row_h[b], row_l[b], *split_bf16(columns))
    values[b, 0] = quads[:128, :128] + quads[128:, 128:]
    values[b, 1] = quads[:128, 128:] - quads[128:, :128]


def tile_place(j):
    y, x, core = j // 8, lax.rem(j // 2, 4), lax.rem(j, 2)
    rows = pl.ds(pl.multiple_of(y * TILE, TILE), TILE)
    cols = pl.ds(pl.multiple_of((lax.rem(x + y, 4) * 2 + core) * TILE, TILE), TILE)
    return rows, cols


def negated(offset):
    return (-offset[0] % 4, -offset[1] % 4, -offset[2] % 2)


def imaging_kernel(
    x_hbm, p_hbm, dual_ref, data_ref, radii_ref, tiles_ref, radius_ref, wave_hbm, wavet_hbm, lanes, subs,
    x_out, p_out, dual_out,
    x_now, p_now, change, slope, p_back, got_change, got_x, got_slope, mixed, halves, x_h, x_l, e_h, e_l,
    adj_h, adj_l, fwd_h, fwd_l, row_h, row_l, rowt_h, rowt_l,
    wave_q, wave_p, waves_q, waves_p,
    duals, error_mid, values, pieces, rad, gains, norm_send, norm_recv, sums, parts,
    local_sems, sends, recvs, z_sends, z_recvs, scatter_sends, scatter_recvs, rad_sems,
    norm_sends, norm_recvs, small_sends, small_recvs,
):
    tabs = (adj_h, adj_l, fwd_h, fwd_l, row_h, row_l, rowt_h, rowt_l)
    me = lax.axis_index("chan")
    facet = lax.axis_index("facet")
    vis = lax.axis_index("vis")
    place = vis * 4 + facet
    at_q = pl.ds(pl.multiple_of(vis * COLS, COLS), COLS)
    at_p = pl.ds(pl.multiple_of(facet * ROWS, ROWS), ROWS)
    loads = [
        pltpu.make_async_copy(source, target, local_sems.at[n])
        for n, (source, target) in enumerate(
            [
                (x_hbm, x_now),
                (p_hbm, p_now),
                (wave_hbm.at[:, :, at_q], wave_q),
                (wave_hbm.at[:, :, at_p], wave_p),
                (wavet_hbm.at[:, at_q, :], waves_q),
                (wavet_hbm.at[:, at_p, :], waves_p),
            ]
        )
    ]
    for copy in loads:
        copy.start()
    entry_barrier()

    def gather_start(source, step):
        copies = []
        for n, offset in enumerate(Z_OFFSETS):
            copies.append(
                remote(source, duals.at[step, place], z_sends.at[step, n], z_recvs.at[step, n], z_device(offset))
            )
            copies[-1].start()
        return copies

    def column_chunk(d):
        return lax.rem(lax.rem(me // 2, 4) + me // 8 + d, 4)

    def chunk_columns(chunk):
        return pl.ds(pl.multiple_of(chunk * CHUNK, CHUNK), CHUNK)

    def adjoint_chunk(chunk):
        return dot3(e_h[...], e_l[...], adj_h[chunk], adj_l[chunk])

    index_of = {offset: n for n, offset in enumerate(OFFSETS)}

    def send(step, source, target, offset):
        n = index_of[offset]
        copy = remote(source, target, sends.at[step, n], recvs.at[step, n], {"chan": chan_peer(offset)})
        copy.start()
        return copy

    def send_tiles(step, image, target, offsets):
        copies = []
        for offset in offsets:
            if offset == (0, 0, 0):
                target[lane_rows(me), :] = image[tile_place(me)]
            else:
                source = image.at[tile_place(chan_peer(offset))]
                copies.append(send(step, source, target.at[lane_rows(me), :], offset))
        return copies

    def send_back(step, target):
        return [send(step, mixed.at[step - 3, lane_rows(chan_peer(offset)), :], target, offset) for offset in OFFSETS]

    def chunk_offsets(d):
        return [(dy, (d - dy) % 4, dc) for dc in range(2) for dy in (1, 3, 0, 2)]

    def scatter_start(step):
        copies = []
        for away in (1, 0):
            side = lax.rem(vis + away, 2)
            for block in range(2):
                measure(side * 2 + block, x_h, x_l, tabs, values)
                for turn in (2, 1, 3, 0) if away else (2, 1, 3):
                    owner = lax.rem(facet + turn, 4)
                    rows = pl.ds(pl.multiple_of(owner * 32, 32), 32)
                    n = turn + 3 if away else turn - 1
                    copies.append(
                        remote(values.at[side * 2 + block, :, rows, :], pieces.at[step, n, block],
                               scatter_sends.at[step, n, block], scatter_recvs.at[step, n, block],
                               {"facet": owner, "vis": side})
                    )
                    copies[-1].start()
        return copies

    def residual(step, copies, dual_now):
        for copy in copies:
            copy.wait()
        own = values[pl.ds(vis * 2, 2), :, pl.ds(pl.multiple_of(facet * 32, 32), 32), :]
        for n in range(7):
            own = own + pieces[step, n]
        return dual_now + own - data_ref[...]

    def gain_of(side, block, squares):
        radius = rad[side, block, 0:1, 0:1]
        gain = 1.0 - radius / jnp.maximum(jnp.sqrt(squares), radius)
        gains[side, block] = jnp.broadcast_to(gain, (8, 128))
        return gain

    def own_gain(block):
        return gains[vis, block, 0:1, :]

    def last_dual(copies):
        now = jnp.stack([error_mid[b] * own_gain(b) for b in range(2)])
        error = residual(1, copies, now)
        squares = jnp.sum((error * error).reshape(2, 8, 8, 128), axis=1)
        norm_send[...] = squares
        copies = []
        for n in range(3):
            copies.append(
                remote(norm_send, norm_recv.at[n], norm_sends.at[n], norm_recvs.at[n], facet_device(n + 1))
            )
            copies[-1].start()
        for copy in copies:
            copy.wait()
        for n in range(3):
            squares = squares + norm_recv[n]
        for b in range(2):
            norm = jnp.sqrt(jnp.sum(squares[b], axis=(0, 1), keepdims=True))
            radius = radii_ref[0, b]
            dual_out[b] = error[b] - error[b] * (radius / jnp.maximum(norm, radius))

    def sum_start(step, value, devices):
        sums[step] = value
        copies = []
        for n, device in enumerate(devices):
            copies.append(
                remote(sums.at[step], parts.at[step, n], small_sends.at[step, n], small_recvs.at[step, n], device)
            )
            copies[-1].start()
        return copies

    def sum_end(step, copies):
        for copy in copies:
            copy.wait()
        value = sums[step]
        for n in range(len(copies)):
            value = value + parts[step, n]
        return value

    group_a = [{"chan": chan_peer(offset)} for offset in GROUP_A]
    group_b = [group_b_device(offset) for offset in GROUP_B]

    gathers = gather_start(dual_ref, 0)
    duals[0, place] = dual_ref[...]
    for b in range(2):
        rad[vis, b] = jnp.full((8, 128), radii_ref[0, b], jnp.float32)
    rad_copy = remote(rad.at[vis], rad.at[vis], rad_sems.at[0], rad_sems.at[1], {"vis": 1 - vis})
    rad_copy.start()
    for copy in loads[:2]:
        copy.wait()

    def subtract(k, carry):
        rows = pl.ds(pl.multiple_of(k * 64, 64), 64)
        change[rows, :] = p_now[rows, :] - x_now[rows, :]
        return carry

    lax.fori_loop(0, ROWS // 64, subtract, 0)
    first = send_tiles(0, change, got_change, OFFSETS + [(0, 0, 0)])
    for copy in loads[2:]:
        copy.wait()
    build_tables(tiles_ref, wave_q, wave_p, waves_q, waves_p, lanes, subs, tabs)
    for copy in gathers:
        copy.wait()
    spread_rows(duals.at[0], None, rowt_h, rowt_l, e_h, e_l)

    for d in (2, 1, 3, 0):
        chunk = column_chunk(d)
        cols = chunk_columns(chunk)
        x = x_now[:, cols]
        x_new = jnp.maximum(0.0, x - step_size * (p_now[:, cols] + adjoint_chunk(chunk)))
        put(x_h, x_l, (slice(None), cols), 2.0 * x_new - x)
        x_now[:, cols] = x_new
    first += send_tiles(1, x_now, got_x, OFFSETS + [(0, 0, 0)])

    error_mid[...] = residual(0, scatter_start(0), dual_ref[...])
    gathers = gather_start(error_mid, 1)
    duals[1, place] = error_mid[...]
    rad_copy.wait()
    for copy in gathers:
        copy.wait()
    spread_rows(duals.at[1], gain_of, rowt_h, rowt_l, e_h, e_l)
    second = []
    for d in (2, 1, 3, 0):
        chunk = column_chunk(d)
        slope[:, chunk_columns(chunk)] = adjoint_chunk(chunk)
        second += send_tiles(2, slope, got_slope, chunk_offsets(d))
    for copy in first:
        copy.wait()
    total = pack(gram_of(lambda rows: got_change[rows, :] + 2.0 * got_x[rows, :], halves))
    small = sum_start(1, sum_end(0, sum_start(0, total, group_a)), group_b)
    total = sum_end(1, small)
    mix_into(mixed.at[0], halves, inverse_root(unpack(total), radius_ref[0]))
    third = send_back(3, p_back.at[me])
    p_back[me] = mixed[0, lane_rows(me), :]
    for copy in second:
        copy.wait()
    total = gram_of(
        lambda rows: jnp.maximum(mixed[0, rows, :] - got_x[rows, :], got_x[rows, :] - got_slope[rows, :]), halves
    )
    total = sum_end(2, sum_start(2, pack(total), group_a))
    total = sum_end(3, sum_start(3, total, group_b))
    mix_into(mixed.at[1], halves, inverse_root(unpack(total), radius_ref[0]))
    rows, cols = tile_place(me)
    p_store = pltpu.make_async_copy(mixed.at[1, lane_rows(me), :], p_out.at[rows, cols], local_sems.at[7])
    p_store.start()
    fourth = send_back(4, p_out.at[rows, cols])

    for n, offset in enumerate(OFFSETS + [(0, 0, 0)]):
        j = chan_peer(negated(offset))
        if n < len(OFFSETS):
            third[n].wait_recv()
        rows, cols = tile_place(j)
        x = x_now[rows, cols]
        x_new = jnp.maximum(0.0, x - step_size * (p_back[j] + slope[rows, cols]))
        put(x_h, x_l, (rows, cols), 2.0 * x_new - x)
        x_now[rows, cols] = x_new
    x_store = pltpu.make_async_copy(x_now, x_out, local_sems.at[6])
    x_store.start()
    last_dual(scatter_start(1))
    for copy in third:
        copy.wait_send()
    x_store.wait()
    p_store.wait()
    for copy in fourth:
        copy.wait()


def store_kernel(x_in, p_in, dual_in, x_out, p_out, dual_out, x_buf, p_buf, dual_buf, load_sems, store_sems):
    moves = []
    for source, buffer, target in ((x_in, x_buf, x_out), (p_in, p_buf, p_out)):
        for k in range(4):
            rows = slice(k * 128, (k + 1) * 128)
            moves.append((source.at[rows], buffer.at[rows], target.at[0, rows]))
    moves.append((dual_in, dual_buf, dual_out.at[0]))
    loads = [pltpu.make_async_copy(a, b, load_sems.at[n]) for n, (a, b, c) in enumerate(moves)]
    stores = [pltpu.make_async_copy(b, c, store_sems.at[n]) for n, (a, b, c) in enumerate(moves)]
    for copy in loads:
        copy.start()
    for load, store in zip(loads, stores):
        load.wait()
        store.start()
    for copy in stores:
        copy.wait()


def on_device(cube, lowrank_dual, vis_dual, visibilities, radii, tiles, facet_radius):
    f32, bf16 = jnp.float32, jnp.bfloat16
    dma = pltpu.SemaphoreType.DMA
    vmem = pl.BlockSpec(memory_space=pltpu.VMEM)
    smem = pl.BlockSpec(memory_space=pltpu.SMEM)
    anywhere = pl.BlockSpec(memory_space=pl.ANY)
    own = vis_dual.shape[1:]
    image = (ROWS, COLS)
    cube_next, lowrank_next, vis_next = pl.pallas_call(
        imaging_kernel,
        out_shape=[
            jax.ShapeDtypeStruct(image, f32),
            jax.ShapeDtypeStruct(image, f32),
            jax.ShapeDtypeStruct(own, f32),
        ],
        in_specs=[anywhere, anywhere, vmem, vmem, smem, smem, smem, anywhere, anywhere, vmem, vmem],
        out_specs=[anywhere, anywhere, vmem],
        scratch_shapes=[
            pltpu.VMEM(image, f32),
            pltpu.VMEM(image, f32),
            pltpu.VMEM(image, f32),
            pltpu.VMEM(image, f32),
            pltpu.VMEM((CHANNELS, TILE, TILE), f32),
            pltpu.VMEM((CHANNELS * PITCH, TILE), f32),
            pltpu.VMEM((CHANNELS * PITCH, TILE), f32),
            pltpu.VMEM((CHANNELS * PITCH, TILE), f32),
            pltpu.VMEM((2, CHANNELS * PITCH, TILE), f32),
            pltpu.VMEM((TILE // 8, 2 * CHANNELS, 1024), bf16),
            pltpu.VMEM(image, bf16),
            pltpu.VMEM(image, bf16),
            pltpu.VMEM(image, bf16),
            pltpu.VMEM(image, bf16),
            pltpu.VMEM((COLS // CHUNK, BLOCKS * 256, CHUNK), bf16),
            pltpu.VMEM((COLS // CHUNK, BLOCKS * 256, CHUNK), bf16),
            pltpu.VMEM((BLOCKS, COLS, 256), bf16),
            pltpu.VMEM((BLOCKS, COLS, 256), bf16),
            pltpu.VMEM((BLOCKS, 256, ROWS), bf16),
            pltpu.VMEM((BLOCKS, 256, ROWS), bf16),
            pltpu.VMEM((BLOCKS, ROWS, 256), bf16),
            pltpu.VMEM((BLOCKS, ROWS, 256), bf16),
            pltpu.VMEM((2, TILE, COLS), f32),
            pltpu.VMEM((2, TILE, ROWS), f32),
            pltpu.VMEM((2, COLS, TILE), f32),
            pltpu.VMEM((2, ROWS, TILE), f32),
            pltpu.VMEM((2, 8) + own, f32),
            pltpu.VMEM(own, f32),
            pltpu.VMEM((BLOCKS, 2, TILE, TILE), f32),
            pltpu.VMEM((2, 7) + own, f32),
            pltpu.VMEM((2, 2, 8, 128), f32),
            pltpu.VMEM((2, 2, 8, 128), f32),
            pltpu.VMEM((2, 8, 128), f32),
            pltpu.VMEM((3, 2, 8, 128), f32),
            pltpu.VMEM((4, 8, 128), f32),
            pltpu.VMEM((4, 7, 8, 128), f32),
            dma((8,)),
            dma((5, 31)),
            dma((5, 31)),
            dma((2, 7)),
            dma((2, 7)),
            dma((2, 7, 2)),
            dma((2, 7, 2)),
            dma((2,)),
            dma((3,)),
            dma((3,)),
            dma((4, 7)),
            dma((4, 7)),
        ],
        compiler_params=pltpu.CompilerParams(
            collective_id=0, has_side_effects=True, vmem_limit_bytes=56 << 20
        ),
        name="imaging",
    )(
        cube[0], lowrank_dual[0], vis_dual[0], visibilities[0], radii, jnp.swapaxes(tiles, 1, 2), facet_radius,
        *[jnp.asarray(value) for value in waves()],
    )
    return pl.pallas_call(
        store_kernel,
        out_shape=[
            jax.ShapeDtypeStruct((1,) + image, f32),
            jax.ShapeDtypeStruct((1,) + image, f32),
            jax.ShapeDtypeStruct((1,) + own, f32),
        ],
        in_specs=[anywhere] * 3,
        out_specs=[anywhere] * 3,
        scratch_shapes=[pltpu.VMEM(image, f32), pltpu.VMEM(image, f32), pltpu.VMEM(own, f32), dma((9,)), dma((9,))],
        compiler_params=pltpu.CompilerParams(vmem_limit_bytes=56 << 20),
        name="store",
    )(cube_next, lowrank_next, vis_next)


def solution(mesh):
    placed = (
        P("chan", "facet", "vis"),
        P("chan", "facet", "vis"),
        P("chan", "vis", None, "facet", None),
        P("chan", "vis", None, "facet", None),
        P("chan", "vis"),
        P("chan", None, None),
        P("facet"),
    )
    return jax.shard_map(
        on_device,
        mesh=mesh,
        in_specs=placed,
        out_specs=(
            P("chan", "facet", "vis"),
            P("chan", "facet", "vis"),
            P("chan", "vis", None, "facet", None),
        ),
        check_vma=False,
    )
```

```python
import functools
import math

import jax
import jax.numpy as jnp
import numpy as np
from jax import lax
from jax.experimental import pallas as pl
from jax.experimental.pallas import tpu as pltpu
from jax.sharding import PartitionSpec as P

IMAGE = 2048
TILE = 128
BLOCKS = 4
NS_STEPS = 10
ITERS = 2
CHANNELS = 32
ROWS = 512
COLS = 1024
CHUNK = 256
PITCH = 136


step_size = 0.5
highest = lax.Precision.HIGHEST


def chan_peer(offset):
    me = lax.axis_index("chan")
    dy, dx, dc = offset
    y = lax.rem(me // 8 + dy, 4)
    x = lax.rem(me // 2 + dx, 4)
    return (y * 4 + x) * 2 + lax.rem(me + dc, 2)


OFFSETS = [
    (3, 3, 1), (2, 3, 0), (2, 2, 0), (1, 3, 1), (3, 1, 1), (3, 2, 1),
    (0, 1, 0), (2, 1, 1), (0, 1, 1), (0, 3, 1), (1, 1, 1), (3, 0, 1),
    (2, 2, 1), (2, 0, 0), (0, 2, 1), (3, 3, 0), (1, 2, 1), (1, 0, 0),
    (0, 0, 1), (0, 2, 0), (1, 0, 1), (2, 1, 0), (3, 0, 0), (2, 3, 1),
    (0, 3, 0), (3, 2, 0), (1, 2, 0), (1, 1, 0), (3, 1, 0), (1, 3, 0),
    (2, 0, 1),
]
GROUP_A = [(0, dx, dc) for dx in (2, 1, 3, 0) for dc in range(2) if (dx, dc) != (0, 0)]
GROUP_B = [(dy, dv) for dv in (1, 0) for dy in (2, 1, 3, 0) if (dy, dv) != (0, 0)]


Z_OFFSETS = (4, 3, 5, 2, 6, 1, 7)


def group_b_device(offset):
    me = lax.axis_index("chan")
    return {
        "chan": lax.rem(me // 8 + offset[0], 4) * 8 + lax.rem(me, 8),
        "vis": lax.rem(lax.axis_index("vis") + offset[1], 2),
    }


def remote(source, target, send_sem, recv_sem, device):
    return pltpu.make_async_remote_copy(
        src_ref=source,
        dst_ref=target,
        send_sem=send_sem,
        recv_sem=recv_sem,
        device_id=device,
        device_id_type=pl.DeviceIdType.MESH,
    )


def split_bf16(value):
    high = value.astype(jnp.bfloat16)
    return high, (value - high.astype(jnp.float32)).astype(jnp.bfloat16)


def z_device(offset):
    z = lax.rem(lax.axis_index("vis") * 4 + lax.axis_index("facet") + offset, 8)
    return {"facet": lax.rem(z, 4), "vis": z // 4}


def facet_device(offset):
    return {"facet": lax.rem(lax.axis_index("facet") + offset, 4)}


def entry_barrier():
    barrier = pltpu.get_barrier_semaphore()
    peers = [{"chan": chan_peer(offset)} for offset in OFFSETS]
    peers += [group_b_device(offset) for offset in GROUP_B if offset[0] and offset[1]]
    peers += [z_device(offset) for offset in Z_OFFSETS]
    for device in peers:
        pl.semaphore_signal(barrier, inc=1, device_id=device, device_id_type=pl.DeviceIdType.MESH)
    pl.semaphore_wait(barrier, len(peers))


def stripes(group):
    return [pl.ds(group * 8 + s, CHANNELS, stride=PITCH) for s in range(8)]


def gram_of(stripe, halves):
    def body(group, total):
        block = jnp.concatenate([stripe(rows) for rows in stripes(group)], axis=1)
        both = jnp.concatenate(split_bf16(block), axis=0)
        halves[group] = both
        return total + lax.dot_general(
            both, both, (((1,), (1,)), ((), ())), preferred_element_type=jnp.float32
        )

    total = lax.fori_loop(
        0, TILE // 8, body, jnp.zeros((2 * CHANNELS, 2 * CHANNELS), jnp.float32), unroll=4
    )
    total = total[:CHANNELS] + total[CHANNELS:]
    return total[:, :CHANNELS] + total[:, CHANNELS:]


def mix_into(target, halves, root):
    high, low = split_bf16(root)
    weights = jnp.concatenate(
        [jnp.concatenate([high, high], axis=1), jnp.concatenate([low, low], axis=1)], axis=0
    )

    def body(group, carry):
        mixed = jnp.dot(weights, halves[group], preferred_element_type=jnp.float32)
        mixed = mixed[:CHANNELS] + mixed[CHANNELS:]
        for s, rows in enumerate(stripes(group)):
            target[rows, :] = mixed[:, s * 128 : (s + 1) * 128]
        return carry

    lax.fori_loop(0, TILE // 8, body, 0, unroll=4)


def matmul(a, b):
    return jnp.dot(a, b, precision=highest, preferred_element_type=jnp.float32)


def inverse_root(gram, radius):
    rows = lax.broadcasted_iota(jnp.int32, gram.shape, 0)
    eye = jnp.where(rows == lax.broadcasted_iota(jnp.int32, gram.shape, 1), 1.0, 0.0)
    matrix = eye + gram / (radius * radius)
    trace = jnp.sum(matrix * eye, axis=(0, 1), keepdims=True)
    current = matrix / trace
    inverse = eye
    for step in range(NS_STEPS):
        product = matmul(inverse, current) if step else current
        middle = 1.5 * eye - 0.5 * product
        inverse = matmul(middle, inverse) if step else middle
        if step < NS_STEPS - 1:
            current = matmul(current, middle)
    return inverse / jnp.sqrt(trace)


def pack(gram):
    return jnp.concatenate([gram[8 * k : 8 * k + 8] for k in range(4)], axis=1)


def unpack(packed):
    return jnp.concatenate([packed[:, 32 * k : 32 * k + 32] for k in range(4)], axis=0)


def lane_rows(index):
    return pl.ds(pl.multiple_of(index * PITCH, 8), TILE)


def waves():
    frequency = np.arange(TILE)
    angle = np.outer(frequency, np.arange(IMAGE)) % IMAGE * (2.0 * math.pi / IMAGE)
    table = np.stack([np.cos(angle), np.sin(angle)]) / math.sqrt(IMAGE)
    turn = np.outer(np.arange(16), np.arange(128)) % 16 * (2.0 * math.pi / 16)
    turns = np.stack([np.cos(turn), np.sin(turn)], axis=1)
    lanes = np.broadcast_to(turns[:, :, None, :], (16, 2, 8, 128))
    subs = np.broadcast_to(turns[:, :, :16, None], (16, 2, 16, 128))
    return [
        np.ascontiguousarray(value, dtype=np.float32)
        for value in (table, table.transpose(0, 2, 1), lanes, subs)
    ]


def turned(cosine, sine, turn, group):
    shape = cosine.shape
    cosine = cosine.reshape(shape[0] // group, group, shape[1])
    sine = sine.reshape(cosine.shape)
    c = cosine * turn[0] - sine * turn[1]
    s = sine * turn[0] + cosine * turn[1]
    return c.reshape(shape), s.reshape(shape)


def put(high_ref, low_ref, where, value):
    high, low = split_bf16(value)
    high_ref[where] = high
    low_ref[where] = low


def dot3(ah, al, bh, bl):
    def dot(a, b):
        return jnp.dot(a, b, preferred_element_type=jnp.float32)

    return dot(ah, bh) + dot(al, bh) + dot(ah, bl)


def build_tables(tiles_ref, wave_q, wave_p, waves_q, waves_p, lanes, subs, tabs):
    adj_h, adj_l, fwd_h, fwd_l, row_h, row_l, rowt_h, rowt_l = tabs

    def body(b, carry):
        turn_u = tiles_ref[0, 0, b]
        turn_v = tiles_ref[0, 1, b]
        lane_v = (lanes[turn_v, 0], lanes[turn_v, 1])
        lane_u = (lanes[turn_u, 0], lanes[turn_u, 1])
        sub_v = (subs[turn_v, 0], subs[turn_v, 1])
        sub_u = (subs[turn_u, 0], subs[turn_u, 1])
        first = pl.ds(pl.multiple_of(b * 256, 256), 128)
        second = pl.ds(pl.multiple_of(b * 256 + 128, 128), 128)
        for k in range(COLS // TILE):
            cols = slice(k * TILE, (k + 1) * TILE)
            half = slice(k % 2 * TILE, (k % 2 + 1) * TILE)
            c, s = turned(wave_q[0, :, cols], wave_q[1, :, cols], lane_v, 8)
            put(adj_h, adj_l, (k // 2, first, half), c)
            put(adj_h, adj_l, (k // 2, second, half), -s)
            c, s = turned(waves_q[0, cols], waves_q[1, cols], sub_v, 16)
            put(fwd_h, fwd_l, (b, cols, slice(0, 128)), c)
            put(fwd_h, fwd_l, (b, cols, slice(128, 256)), -s)
        for k in range(ROWS // TILE):
            cols = slice(k * TILE, (k + 1) * TILE)
            c, s = turned(wave_p[0, :, cols], wave_p[1, :, cols], lane_u, 8)
            put(row_h, row_l, (b, slice(0, 128), cols), c)
            put(row_h, row_l, (b, slice(128, 256), cols), s)
            c, s = turned(waves_p[0, cols], waves_p[1, cols], sub_u, 16)
            put(rowt_h, rowt_l, (b, cols, slice(0, 128)), c)
            put(rowt_h, rowt_l, (b, cols, slice(128, 256)), s)
        return carry

    lax.fori_loop(0, BLOCKS, body, 0)


def spread_rows(duals, gain_of, rowt_h, rowt_l, e_h, e_l):
    def body(b, carry):
        side, block = b // 2, b % 2
        real = jnp.concatenate([duals[4 * side + f, block, 0] for f in range(4)], axis=0)
        imag = jnp.concatenate([duals[4 * side + f, block, 1] for f in range(4)], axis=0)
        if gain_of is not None:
            gain = gain_of(side, block, jnp.sum(real * real + imag * imag, axis=(0, 1), keepdims=True))
            real, imag = real * gain, imag * gain
        both = jnp.concatenate(
            [jnp.concatenate([real, imag], axis=1), jnp.concatenate([-imag, real], axis=1)], axis=0
        )
        spread = dot3(rowt_h[b], rowt_l[b], *split_bf16(both))
        put(e_h, e_l, (slice(None), pl.ds(pl.multiple_of(b * 256, 256), 256)), spread)
        return carry

    lax.fori_loop(0, BLOCKS, body, 0)


def measure(b, x_h, x_l, tabs, values):
    adj_h, adj_l, fwd_h, fwd_l, row_h, row_l, rowt_h, rowt_l = tabs
    columns = dot3(x_h[...], x_l[...], fwd_h[b], fwd_l[b])
    quads = dot3(row_h[b], row_l[b], *split_bf16(columns))
    values[b, 0] = quads[:128, :128] + quads[128:, 128:]
    values[b, 1] = quads[:128, 128:] - quads[128:, :128]


def tile_place(j):
    y, x, core = j // 8, lax.rem(j // 2, 4), lax.rem(j, 2)
    rows = pl.ds(pl.multiple_of(y * TILE, TILE), TILE)
    cols = pl.ds(pl.multiple_of((lax.rem(x + y, 4) * 2 + core) * TILE, TILE), TILE)
    return rows, cols


def negated(offset):
    return (-offset[0] % 4, -offset[1] % 4, -offset[2] % 2)


def imaging_kernel(
    x_hbm, p_hbm, dual_ref, data_ref, radii_ref, tiles_ref, radius_ref, wave_hbm, wavet_hbm, lanes, subs,
    x_out, p_out, dual_out,
    x_now, p_now, change, slope, p_back, got_change, got_x, got_slope, mixed, halves, x_h, x_l, e_h, e_l,
    adj_h, adj_l, fwd_h, fwd_l, row_h, row_l, rowt_h, rowt_l,
    wave_q, wave_p, waves_q, waves_p,
    duals, error_mid, values, pieces, rad, gains, norm_send, norm_recv, sums, parts,
    local_sems, sends, recvs, z_sends, z_recvs, scatter_sends, scatter_recvs, rad_sems,
    norm_sends, norm_recvs, small_sends, small_recvs,
):
    tabs = (adj_h, adj_l, fwd_h, fwd_l, row_h, row_l, rowt_h, rowt_l)
    me = lax.axis_index("chan")
    facet = lax.axis_index("facet")
    vis = lax.axis_index("vis")
    place = vis * 4 + facet
    at_q = pl.ds(pl.multiple_of(vis * COLS, COLS), COLS)
    at_p = pl.ds(pl.multiple_of(facet * ROWS, ROWS), ROWS)
    loads = [
        pltpu.make_async_copy(source, target, local_sems.at[n])
        for n, (source, target) in enumerate(
            [
                (x_hbm, x_now),
                (p_hbm, p_now),
                (wave_hbm.at[:, :, at_q], wave_q),
                (wave_hbm.at[:, :, at_p], wave_p),
                (wavet_hbm.at[:, at_q, :], waves_q),
                (wavet_hbm.at[:, at_p, :], waves_p),
            ]
        )
    ]
    for copy in loads:
        copy.start()
    entry_barrier()

    def gather_start(source, step):
        copies = []
        for n, offset in enumerate(Z_OFFSETS):
            copies.append(
                remote(source, duals.at[step, place], z_sends.at[step, n], z_recvs.at[step, n], z_device(offset))
            )
            copies[-1].start()
        return copies

    def column_chunk(d):
        return lax.rem(lax.rem(me // 2, 4) + me // 8 + d, 4)

    def chunk_columns(chunk):
        return pl.ds(pl.multiple_of(chunk * CHUNK, CHUNK), CHUNK)

    def adjoint_chunk(chunk):
        return dot3(e_h[...], e_l[...], adj_h[chunk], adj_l[chunk])

    index_of = {offset: n for n, offset in enumerate(OFFSETS)}

    def send(step, source, target, offset):
        n = index_of[offset]
        copy = remote(source, target, sends.at[step, n], recvs.at[step, n], {"chan": chan_peer(offset)})
        copy.start()
        return copy

    def send_tiles(step, image, target, offsets):
        copies = []
        for offset in offsets:
            if offset == (0, 0, 0):
                target[lane_rows(me), :] = image[tile_place(me)]
            else:
                source = image.at[tile_place(chan_peer(offset))]
                copies.append(send(step, source, target.at[lane_rows(me), :], offset))
        return copies

    def send_back(step, target, offsets):
        return [send(step, mixed.at[step - 3, lane_rows(chan_peer(offset)), :], target, offset) for offset in offsets]

    def scatter_start(step):
        copies = []
        for away in (1, 0):
            side = lax.rem(vis + away, 2)
            for block in range(2):
                measure(side * 2 + block, x_h, x_l, tabs, values)
                for turn in (2, 1, 3, 0) if away else (2, 1, 3):
                    owner = lax.rem(facet + turn, 4)
                    rows = pl.ds(pl.multiple_of(owner * 32, 32), 32)
                    n = turn + 3 if away else turn - 1
                    copies.append(
                        remote(values.at[side * 2 + block, :, rows, :], pieces.at[step, n, block],
                               scatter_sends.at[step, n, block], scatter_recvs.at[step, n, block],
                               {"facet": owner, "vis": side})
                    )
                    copies[-1].start()
        return copies

    def residual(step, copies, dual_now):
        for copy in copies:
            copy.wait()
        own = values[pl.ds(vis * 2, 2), :, pl.ds(pl.multiple_of(facet * 32, 32), 32), :]
        for n in range(7):
            own = own + pieces[step, n]
        return dual_now + own - data_ref[...]

    def gain_of(side, block, squares):
        radius = rad[side, block, 0:1, 0:1]
        gain = 1.0 - radius / jnp.maximum(jnp.sqrt(squares), radius)
        gains[side, block] = jnp.broadcast_to(gain, (8, 128))
        return gain

    def own_gain(block):
        return gains[vis, block, 0:1, :]

    def last_dual(copies):
        now = jnp.stack([error_mid[b] * own_gain(b) for b in range(2)])
        error = residual(1, copies, now)
        squares = jnp.sum((error * error).reshape(2, 8, 8, 128), axis=1)
        norm_send[...] = squares
        copies = []
        for n in range(3):
            copies.append(
                remote(norm_send, norm_recv.at[n], norm_sends.at[n], norm_recvs.at[n], facet_device(n + 1))
            )
            copies[-1].start()
        for copy in copies:
            copy.wait()
        for n in range(3):
            squares = squares + norm_recv[n]
        for b in range(2):
            norm = jnp.sqrt(jnp.sum(squares[b], axis=(0, 1), keepdims=True))
            radius = radii_ref[0, b]
            dual_out[b] = error[b] - error[b] * (radius / jnp.maximum(norm, radius))

    def sum_start(step, value, devices):
        sums[step] = value
        copies = []
        for n, device in enumerate(devices):
            copies.append(
                remote(sums.at[step], parts.at[step, n], small_sends.at[step, n], small_recvs.at[step, n], device)
            )
            copies[-1].start()
        return copies

    def sum_end(step, copies):
        for copy in copies:
            copy.wait()
        value = sums[step]
        for n in range(len(copies)):
            value = value + parts[step, n]
        return value

    group_a = [{"chan": chan_peer(offset)} for offset in GROUP_A]
    group_b = [group_b_device(offset) for offset in GROUP_B]

    gathers = gather_start(dual_ref, 0)
    duals[0, place] = dual_ref[...]
    for b in range(2):
        rad[vis, b] = jnp.full((8, 128), radii_ref[0, b], jnp.float32)
    rad_copy = remote(rad.at[vis], rad.at[vis], rad_sems.at[0], rad_sems.at[1], {"vis": 1 - vis})
    rad_copy.start()
    for copy in loads[:2]:
        copy.wait()

    def subtract(k, carry):
        rows = pl.ds(pl.multiple_of(k * 64, 64), 64)
        change[rows, :] = p_now[rows, :] - x_now[rows, :]
        return carry

    lax.fori_loop(0, ROWS // 64, subtract, 0)
    first = send_tiles(0, change, got_change, OFFSETS + [(0, 0, 0)])
    for copy in loads[2:]:
        copy.wait()
    build_tables(tiles_ref, wave_q, wave_p, waves_q, waves_p, lanes, subs, tabs)
    for copy in gathers:
        copy.wait()
    spread_rows(duals.at[0], None, rowt_h, rowt_l, e_h, e_l)

    for d in (2, 1, 3, 0):
        chunk = column_chunk(d)
        cols = chunk_columns(chunk)
        x = x_now[:, cols]
        x_new = jnp.maximum(0.0, x - step_size * (p_now[:, cols] + adjoint_chunk(chunk)))
        put(x_h, x_l, (slice(None), cols), 2.0 * x_new - x)
        x_now[:, cols] = x_new
    first += send_tiles(1, x_now, got_x, OFFSETS + [(0, 0, 0)])

    error_mid[...] = residual(0, scatter_start(0), dual_ref[...])
    gathers = gather_start(error_mid, 1)
    duals[1, place] = error_mid[...]
    rad_copy.wait()
    for copy in first:
        copy.wait()
    total = pack(gram_of(lambda rows: got_change[rows, :] + 2.0 * got_x[rows, :], halves))
    small = sum_start(0, total, group_a)
    for copy in gathers:
        copy.wait()
    spread_rows(duals.at[1], gain_of, rowt_h, rowt_l, e_h, e_l)
    small = sum_start(1, sum_end(0, small), group_b)

    def next_gradient(chunk, carry):
        slope[:, chunk_columns(chunk)] = adjoint_chunk(chunk)
        return carry

    lax.fori_loop(0, COLS // CHUNK, next_gradient, 0)
    total = sum_end(1, small)
    second = send_tiles(2, slope, got_slope, OFFSETS + [(0, 0, 0)])
    mix_into(mixed.at[0], halves, inverse_root(unpack(total), radius_ref[0]))
    third = send_back(3, p_back.at[me], OFFSETS[:8])
    p_back[me] = mixed[0, lane_rows(me), :]
    for copy in second:
        copy.wait()
    total = gram_of(
        lambda rows: jnp.maximum(mixed[0, rows, :] - got_x[rows, :], got_x[rows, :] - got_slope[rows, :]), halves
    )
    small = sum_start(2, pack(total), group_a)
    third += send_back(3, p_back.at[me], OFFSETS[8:14])
    small = sum_start(3, sum_end(2, small), group_b)
    third += send_back(3, p_back.at[me], OFFSETS[14:20])
    total = sum_end(3, small)
    third += send_back(3, p_back.at[me], OFFSETS[20:])
    mix_into(mixed.at[1], halves, inverse_root(unpack(total), radius_ref[0]))
    rows, cols = tile_place(me)
    p_store = pltpu.make_async_copy(mixed.at[1, lane_rows(me), :], p_out.at[rows, cols], local_sems.at[7])
    p_store.start()
    fourth = send_back(4, p_out.at[rows, cols], OFFSETS)

    for n, offset in enumerate(OFFSETS + [(0, 0, 0)]):
        j = chan_peer(negated(offset))
        if n < len(OFFSETS):
            third[n].wait_recv()
        rows, cols = tile_place(j)
        x = x_now[rows, cols]
        x_new = jnp.maximum(0.0, x - step_size * (p_back[j] + slope[rows, cols]))
        put(x_h, x_l, (rows, cols), 2.0 * x_new - x)
        x_now[rows, cols] = x_new
    x_store = pltpu.make_async_copy(x_now, x_out, local_sems.at[6])
    x_store.start()
    last_dual(scatter_start(1))
    for copy in third:
        copy.wait_send()
    x_store.wait()
    p_store.wait()
    for copy in fourth:
        copy.wait()


def store_kernel(x_in, p_in, dual_in, x_out, p_out, dual_out, x_buf, p_buf, dual_buf, load_sems, store_sems):
    moves = []
    for source, buffer, target in ((x_in, x_buf, x_out), (p_in, p_buf, p_out)):
        for k in range(4):
            rows = slice(k * 128, (k + 1) * 128)
            moves.append((source.at[rows], buffer.at[rows], target.at[0, rows]))
    moves.append((dual_in, dual_buf, dual_out.at[0]))
    loads = [pltpu.make_async_copy(a, b, load_sems.at[n]) for n, (a, b, c) in enumerate(moves)]
    stores = [pltpu.make_async_copy(b, c, store_sems.at[n]) for n, (a, b, c) in enumerate(moves)]
    for copy in loads:
        copy.start()
    for load, store in zip(loads, stores):
        load.wait()
        store.start()
    for copy in stores:
        copy.wait()


def on_device(cube, lowrank_dual, vis_dual, visibilities, radii, tiles, facet_radius):
    f32, bf16 = jnp.float32, jnp.bfloat16
    dma = pltpu.SemaphoreType.DMA
    vmem = pl.BlockSpec(memory_space=pltpu.VMEM)
    smem = pl.BlockSpec(memory_space=pltpu.SMEM)
    anywhere = pl.BlockSpec(memory_space=pl.ANY)
    own = vis_dual.shape[1:]
    image = (ROWS, COLS)
    cube_next, lowrank_next, vis_next = pl.pallas_call(
        imaging_kernel,
        out_shape=[
            jax.ShapeDtypeStruct(image, f32),
            jax.ShapeDtypeStruct(image, f32),
            jax.ShapeDtypeStruct(own, f32),
        ],
        in_specs=[anywhere, anywhere, vmem, vmem, smem, smem, smem, anywhere, anywhere, vmem, vmem],
        out_specs=[anywhere, anywhere, vmem],
        scratch_shapes=[
            pltpu.VMEM(image, f32),
            pltpu.VMEM(image, f32),
            pltpu.VMEM(image, f32),
            pltpu.VMEM(image, f32),
            pltpu.VMEM((CHANNELS, TILE, TILE), f32),
            pltpu.VMEM((CHANNELS * PITCH, TILE), f32),
            pltpu.VMEM((CHANNELS * PITCH, TILE), f32),
            pltpu.VMEM((CHANNELS * PITCH, TILE), f32),
            pltpu.VMEM((2, CHANNELS * PITCH, TILE), f32),
            pltpu.VMEM((TILE // 8, 2 * CHANNELS, 1024), bf16),
            pltpu.VMEM(image, bf16),
            pltpu.VMEM(image, bf16),
            pltpu.VMEM(image, bf16),
            pltpu.VMEM(image, bf16),
            pltpu.VMEM((COLS // CHUNK, BLOCKS * 256, CHUNK), bf16),
            pltpu.VMEM((COLS // CHUNK, BLOCKS * 256, CHUNK), bf16),
            pltpu.VMEM((BLOCKS, COLS, 256), bf16),
            pltpu.VMEM((BLOCKS, COLS, 256), bf16),
            pltpu.VMEM((BLOCKS, 256, ROWS), bf16),
            pltpu.VMEM((BLOCKS, 256, ROWS), bf16),
            pltpu.VMEM((BLOCKS, ROWS, 256), bf16),
            pltpu.VMEM((BLOCKS, ROWS, 256), bf16),
            pltpu.VMEM((2, TILE, COLS), f32),
            pltpu.VMEM((2, TILE, ROWS), f32),
            pltpu.VMEM((2, COLS, TILE), f32),
            pltpu.VMEM((2, ROWS, TILE), f32),
            pltpu.VMEM((2, 8) + own, f32),
            pltpu.VMEM(own, f32),
            pltpu.VMEM((BLOCKS, 2, TILE, TILE), f32),
            pltpu.VMEM((2, 7) + own, f32),
            pltpu.VMEM((2, 2, 8, 128), f32),
            pltpu.VMEM((2, 2, 8, 128), f32),
            pltpu.VMEM((2, 8, 128), f32),
            pltpu.VMEM((3, 2, 8, 128), f32),
            pltpu.VMEM((4, 8, 128), f32),
            pltpu.VMEM((4, 7, 8, 128), f32),
            dma((8,)),
            dma((5, 31)),
            dma((5, 31)),
            dma((2, 7)),
            dma((2, 7)),
            dma((2, 7, 2)),
            dma((2, 7, 2)),
            dma((2,)),
            dma((3,)),
            dma((3,)),
            dma((4, 7)),
            dma((4, 7)),
        ],
        compiler_params=pltpu.CompilerParams(
            collective_id=0, has_side_effects=True, vmem_limit_bytes=56 << 20
        ),
        name="imaging",
    )(
        cube[0], lowrank_dual[0], vis_dual[0], visibilities[0], radii, jnp.swapaxes(tiles, 1, 2), facet_radius,
        *[jnp.asarray(value) for value in waves()],
    )
    return pl.pallas_call(
        store_kernel,
        out_shape=[
            jax.ShapeDtypeStruct((1,) + image, f32),
            jax.ShapeDtypeStruct((1,) + image, f32),
            jax.ShapeDtypeStruct((1,) + own, f32),
        ],
        in_specs=[anywhere] * 3,
        out_specs=[anywhere] * 3,
        scratch_shapes=[pltpu.VMEM(image, f32), pltpu.VMEM(image, f32), pltpu.VMEM(own, f32), dma((9,)), dma((9,))],
        compiler_params=pltpu.CompilerParams(vmem_limit_bytes=56 << 20),
        name="store",
    )(cube_next, lowrank_next, vis_next)


def solution(mesh):
    placed = (
        P("chan", "facet", "vis"),
        P("chan", "facet", "vis"),
        P("chan", "vis", None, "facet", None),
        P("chan", "vis", None, "facet", None),
        P("chan", "vis"),
        P("chan", None, None),
        P("facet"),
    )
    return jax.shard_map(
        on_device,
        mesh=mesh,
        in_specs=placed,
        out_specs=(
            P("chan", "facet", "vis"),
            P("chan", "facet", "vis"),
            P("chan", "vis", None, "facet", None),
        ),
        check_vma=False,
    )
```

```python
import functools
import math

import jax
import jax.numpy as jnp
import numpy as np
from jax import lax
from jax.experimental import pallas as pl
from jax.experimental.pallas import tpu as pltpu
from jax.sharding import PartitionSpec as P

IMAGE = 2048
TILE = 128
BLOCKS = 4
NS_STEPS = 10
ITERS = 2
CHANNELS = 32
ROWS = 512
COLS = 1024
CHUNK = 256
PITCH = 136


step_size = 0.5
highest = lax.Precision.HIGHEST


def chan_peer(offset):
    me = lax.axis_index("chan")
    dy, dx, dc = offset
    y = lax.rem(me // 8 + dy, 4)
    x = lax.rem(me // 2 + dx, 4)
    return (y * 4 + x) * 2 + lax.rem(me + dc, 2)


OFFSETS = [
    (3, 3, 1), (2, 3, 0), (2, 2, 0), (1, 3, 1), (3, 1, 1), (3, 2, 1),
    (0, 1, 0), (2, 1, 1), (0, 1, 1), (0, 3, 1), (1, 1, 1), (3, 0, 1),
    (2, 2, 1), (2, 0, 0), (0, 2, 1), (3, 3, 0), (1, 2, 1), (1, 0, 0),
    (0, 0, 1), (0, 2, 0), (1, 0, 1), (2, 1, 0), (3, 0, 0), (2, 3, 1),
    (0, 3, 0), (3, 2, 0), (1, 2, 0), (1, 1, 0), (3, 1, 0), (1, 3, 0),
    (2, 0, 1),
]
GROUP_A = [(0, dx, dc) for dx in (2, 1, 3, 0) for dc in range(2) if (dx, dc) != (0, 0)]
GROUP_B = [(dy, dv) for dv in (1, 0) for dy in (2, 1, 3, 0) if (dy, dv) != (0, 0)]


Z_OFFSETS = (4, 3, 5, 2, 6, 1, 7)


def group_b_device(offset):
    me = lax.axis_index("chan")
    return {
        "chan": lax.rem(me // 8 + offset[0], 4) * 8 + lax.rem(me, 8),
        "vis": lax.rem(lax.axis_index("vis") + offset[1], 2),
    }


def remote(source, target, send_sem, recv_sem, device):
    return pltpu.make_async_remote_copy(
        src_ref=source,
        dst_ref=target,
        send_sem=send_sem,
        recv_sem=recv_sem,
        device_id=device,
        device_id_type=pl.DeviceIdType.MESH,
    )


def split_bf16(value):
    high = value.astype(jnp.bfloat16)
    return high, (value - high.astype(jnp.float32)).astype(jnp.bfloat16)


def z_device(offset):
    z = lax.rem(lax.axis_index("vis") * 4 + lax.axis_index("facet") + offset, 8)
    return {"facet": lax.rem(z, 4), "vis": z // 4}


def facet_device(offset):
    return {"facet": lax.rem(lax.axis_index("facet") + offset, 4)}


def entry_barrier():
    barrier = pltpu.get_barrier_semaphore()
    peers = [{"chan": chan_peer(offset)} for offset in OFFSETS]
    peers += [group_b_device(offset) for offset in GROUP_B if offset[0] and offset[1]]
    peers += [z_device(offset) for offset in Z_OFFSETS]
    for device in peers:
        pl.semaphore_signal(barrier, inc=1, device_id=device, device_id_type=pl.DeviceIdType.MESH)
    pl.semaphore_wait(barrier, len(peers))


def stripes(group):
    return [pl.ds(group * 8 + s, CHANNELS, stride=PITCH) for s in range(8)]


def gram_of(stripe, halves):
    def body(group, total):
        block = jnp.concatenate([stripe(rows) for rows in stripes(group)], axis=1)
        both = jnp.concatenate(split_bf16(block), axis=0)
        halves[group] = both
        return total + lax.dot_general(
            both, both, (((1,), (1,)), ((), ())), preferred_element_type=jnp.float32
        )

    total = lax.fori_loop(
        0, TILE // 8, body, jnp.zeros((2 * CHANNELS, 2 * CHANNELS), jnp.float32), unroll=4
    )
    total = total[:CHANNELS] + total[CHANNELS:]
    return total[:, :CHANNELS] + total[:, CHANNELS:]


def mix_into(target, halves, root):
    high, low = split_bf16(root)
    weights = jnp.concatenate(
        [jnp.concatenate([high, high], axis=1), jnp.concatenate([low, low], axis=1)], axis=0
    )

    def body(group, carry):
        mixed = jnp.dot(weights, halves[group], preferred_element_type=jnp.float32)
        mixed = mixed[:CHANNELS] + mixed[CHANNELS:]
        for s, rows in enumerate(stripes(group)):
            target[rows, :] = mixed[:, s * 128 : (s + 1) * 128]
        return carry

    lax.fori_loop(0, TILE // 8, body, 0, unroll=4)


def matmul(a, b):
    return jnp.dot(a, b, precision=highest, preferred_element_type=jnp.float32)


def inverse_root(gram, radius):
    rows = lax.broadcasted_iota(jnp.int32, gram.shape, 0)
    eye = jnp.where(rows == lax.broadcasted_iota(jnp.int32, gram.shape, 1), 1.0, 0.0)
    matrix = eye + gram / (radius * radius)
    trace = jnp.sum(matrix * eye, axis=(0, 1), keepdims=True)
    current = matrix / trace
    inverse = eye
    for step in range(NS_STEPS):
        product = matmul(inverse, current) if step else current
        middle = 1.5 * eye - 0.5 * product
        inverse = matmul(middle, inverse) if step else middle
        if step < NS_STEPS - 1:
            current = matmul(current, middle)
    return inverse / jnp.sqrt(trace)


def pack(gram):
    return jnp.concatenate([gram[8 * k : 8 * k + 8] for k in range(4)], axis=1)


def unpack(packed):
    return jnp.concatenate([packed[:, 32 * k : 32 * k + 32] for k in range(4)], axis=0)


def lane_rows(index):
    return pl.ds(pl.multiple_of(index * PITCH, 8), TILE)


def waves():
    frequency = np.arange(TILE)
    angle = np.outer(frequency, np.arange(IMAGE)) % IMAGE * (2.0 * math.pi / IMAGE)
    table = np.stack([np.cos(angle), np.sin(angle)]) / math.sqrt(IMAGE)
    turn = np.outer(np.arange(16), np.arange(128)) % 16 * (2.0 * math.pi / 16)
    turns = np.stack([np.cos(turn), np.sin(turn)], axis=1)
    lanes = np.broadcast_to(turns[:, :, None, :], (16, 2, 8, 128))
    subs = np.broadcast_to(turns[:, :, :16, None], (16, 2, 16, 128))
    return [
        np.ascontiguousarray(value, dtype=np.float32)
        for value in (table, table.transpose(0, 2, 1), lanes, subs)
    ]


def turned(cosine, sine, turn, group):
    shape = cosine.shape
    cosine = cosine.reshape(shape[0] // group, group, shape[1])
    sine = sine.reshape(cosine.shape)
    c = cosine * turn[0] - sine * turn[1]
    s = sine * turn[0] + cosine * turn[1]
    return c.reshape(shape), s.reshape(shape)


def put(high_ref, low_ref, where, value):
    high, low = split_bf16(value)
    high_ref[where] = high
    low_ref[where] = low


def dot3(ah, al, bh, bl):
    def dot(a, b):
        return jnp.dot(a, b, preferred_element_type=jnp.float32)

    return dot(ah, bh) + dot(al, bh) + dot(ah, bl)


def build_tables(tiles_ref, wave_q, wave_p, waves_q, waves_p, lanes, subs, tabs):
    adj_h, adj_l, fwd_h, fwd_l, row_h, row_l, rowt_h, rowt_l = tabs

    def body(b, carry):
        turn_u = tiles_ref[0, 0, b]
        turn_v = tiles_ref[0, 1, b]
        lane_v = (lanes[turn_v, 0], lanes[turn_v, 1])
        lane_u = (lanes[turn_u, 0], lanes[turn_u, 1])
        sub_v = (subs[turn_v, 0], subs[turn_v, 1])
        sub_u = (subs[turn_u, 0], subs[turn_u, 1])
        first = pl.ds(pl.multiple_of(b * 256, 256), 128)
        second = pl.ds(pl.multiple_of(b * 256 + 128, 128), 128)
        for k in range(COLS // TILE):
            cols = slice(k * TILE, (k + 1) * TILE)
            half = slice(k % 2 * TILE, (k % 2 + 1) * TILE)
            c, s = turned(wave_q[0, :, cols], wave_q[1, :, cols], lane_v, 8)
            put(adj_h, adj_l, (k // 2, first, half), c)
            put(adj_h, adj_l, (k // 2, second, half), -s)
            c, s = turned(waves_q[0, cols], waves_q[1, cols], sub_v, 16)
            put(fwd_h, fwd_l, (b, cols, slice(0, 128)), c)
            put(fwd_h, fwd_l, (b, cols, slice(128, 256)), -s)
        for k in range(ROWS // TILE):
            cols = slice(k * TILE, (k + 1) * TILE)
            c, s = turned(wave_p[0, :, cols], wave_p[1, :, cols], lane_u, 8)
            put(row_h, row_l, (b, slice(0, 128), cols), c)
            put(row_h, row_l, (b, slice(128, 256), cols), s)
            c, s = turned(waves_p[0, cols], waves_p[1, cols], sub_u, 16)
            put(rowt_h, rowt_l, (b, cols, slice(0, 128)), c)
            put(rowt_h, rowt_l, (b, cols, slice(128, 256)), s)
        return carry

    lax.fori_loop(0, BLOCKS, body, 0)


def spread_rows(duals, gain_of, rowt_h, rowt_l, e_h, e_l):
    def body(b, carry):
        side, block = b // 2, b % 2
        real = jnp.concatenate([duals[4 * side + f, block, 0] for f in range(4)], axis=0)
        imag = jnp.concatenate([duals[4 * side + f, block, 1] for f in range(4)], axis=0)
        if gain_of is not None:
            gain = gain_of(side, block, jnp.sum(real * real + imag * imag, axis=(0, 1), keepdims=True))
            real, imag = real * gain, imag * gain
        both = jnp.concatenate(
            [jnp.concatenate([real, imag], axis=1), jnp.concatenate([-imag, real], axis=1)], axis=0
        )
        spread = dot3(rowt_h[b], rowt_l[b], *split_bf16(both))
        put(e_h, e_l, (slice(None), pl.ds(pl.multiple_of(b * 256, 256), 256)), spread)
        return carry

    lax.fori_loop(0, BLOCKS, body, 0)


def measure(b, x_h, x_l, tabs, values):
    adj_h, adj_l, fwd_h, fwd_l, row_h, row_l, rowt_h, rowt_l = tabs
    columns = dot3(x_h[...], x_l[...], fwd_h[b], fwd_l[b])
    quads = dot3(row_h[b], row_l[b], *split_bf16(columns))
    values[b, 0] = quads[:128, :128] + quads[128:, 128:]
    values[b, 1] = quads[:128, 128:] - quads[128:, :128]


def tile_place(j):
    y, x, core = j // 8, lax.rem(j // 2, 4), lax.rem(j, 2)
    rows = pl.ds(pl.multiple_of(y * TILE, TILE), TILE)
    cols = pl.ds(pl.multiple_of((lax.rem(x + y, 4) * 2 + core) * TILE, TILE), TILE)
    return rows, cols


def negated(offset):
    return (-offset[0] % 4, -offset[1] % 4, -offset[2] % 2)


def imaging_kernel(
    x_hbm, p_hbm, dual_ref, data_ref, radii_ref, tiles_ref, radius_ref, wave_hbm, wavet_hbm, lanes, subs,
    x_out, p_out, dual_out,
    x_now, p_now, change, slope, p_back, got_change, got_x, got_slope, mixed, halves, x_h, x_l, e_h, e_l,
    adj_h, adj_l, fwd_h, fwd_l, row_h, row_l, rowt_h, rowt_l,
    wave_q, wave_p, waves_q, waves_p,
    duals, error_mid, values, pieces, rad, gains, norm_send, norm_recv, sums, parts,
    local_sems, sends, recvs, z_sends, z_recvs, scatter_sends, scatter_recvs, rad_sems,
    norm_sends, norm_recvs, small_sends, small_recvs,
):
    tabs = (adj_h, adj_l, fwd_h, fwd_l, row_h, row_l, rowt_h, rowt_l)
    me = lax.axis_index("chan")
    facet = lax.axis_index("facet")
    vis = lax.axis_index("vis")
    place = vis * 4 + facet
    at_q = pl.ds(pl.multiple_of(vis * COLS, COLS), COLS)
    at_p = pl.ds(pl.multiple_of(facet * ROWS, ROWS), ROWS)
    loads = [
        pltpu.make_async_copy(source, target, local_sems.at[n])
        for n, (source, target) in enumerate(
            [
                (x_hbm, x_now),
                (p_hbm, p_now),
                (wave_hbm.at[:, :, at_q], wave_q),
                (wave_hbm.at[:, :, at_p], wave_p),
                (wavet_hbm.at[:, at_q, :], waves_q),
                (wavet_hbm.at[:, at_p, :], waves_p),
            ]
        )
    ]
    for copy in loads:
        copy.start()
    entry_barrier()

    def gather_start(source, step):
        copies = []
        for n, offset in enumerate(Z_OFFSETS):
            copies.append(
                remote(source, duals.at[step, place], z_sends.at[step, n], z_recvs.at[step, n], z_device(offset))
            )
            copies[-1].start()
        return copies

    def column_chunk(d):
        return lax.rem(lax.rem(me // 2, 4) + me // 8 + d, 4)

    def chunk_columns(chunk):
        return pl.ds(pl.multiple_of(chunk * CHUNK, CHUNK), CHUNK)

    def adjoint_chunk(chunk):
        return dot3(e_h[...], e_l[...], adj_h[chunk], adj_l[chunk])

    index_of = {offset: n for n, offset in enumerate(OFFSETS)}

    def send(step, source, target, offset):
        n = index_of[offset]
        copy = remote(source, target, sends.at[step, n], recvs.at[step, n], {"chan": chan_peer(offset)})
        copy.start()
        return copy

    def send_tiles(step, image, target, offsets):
        copies = []
        for offset in offsets:
            if offset == (0, 0, 0):
                target[lane_rows(me), :] = image[tile_place(me)]
            else:
                source = image.at[tile_place(chan_peer(offset))]
                copies.append(send(step, source, target.at[lane_rows(me), :], offset))
        return copies

    def send_back(step, target, offsets):
        return [send(step, mixed.at[step - 3, lane_rows(chan_peer(offset)), :], target, offset) for offset in offsets]

    def chunk_offsets(d):
        return [(dy, (d - dy) % 4, dc) for dc in range(2) for dy in (1, 3, 0, 2)]

    def scatter_start(step):
        copies = []
        for away in (1, 0):
            side = lax.rem(vis + away, 2)
            for block in range(2):
                measure(side * 2 + block, x_h, x_l, tabs, values)
                for turn in (2, 1, 3, 0) if away else (2, 1, 3):
                    owner = lax.rem(facet + turn, 4)
                    rows = pl.ds(pl.multiple_of(owner * 32, 32), 32)
                    n = turn + 3 if away else turn - 1
                    copies.append(
                        remote(values.at[side * 2 + block, :, rows, :], pieces.at[step, n, block],
                               scatter_sends.at[step, n, block], scatter_recvs.at[step, n, block],
                               {"facet": owner, "vis": side})
                    )
                    copies[-1].start()
        return copies

    def residual(step, copies, dual_now):
        for copy in copies:
            copy.wait()
        own = values[pl.ds(vis * 2, 2), :, pl.ds(pl.multiple_of(facet * 32, 32), 32), :]
        for n in range(7):
            own = own + pieces[step, n]
        return dual_now + own - data_ref[...]

    def gain_of(side, block, squares):
        radius = rad[side, block, 0:1, 0:1]
        gain = 1.0 - radius / jnp.maximum(jnp.sqrt(squares), radius)
        gains[side, block] = jnp.broadcast_to(gain, (8, 128))
        return gain

    def own_gain(block):
        return gains[vis, block, 0:1, :]

    def last_dual(copies):
        now = jnp.stack([error_mid[b] * own_gain(b) for b in range(2)])
        error = residual(1, copies, now)
        squares = jnp.sum((error * error).reshape(2, 8, 8, 128), axis=1)
        norm_send[...] = squares
        copies = []
        for n in range(3):
            copies.append(
                remote(norm_send, norm_recv.at[n], norm_sends.at[n], norm_recvs.at[n], facet_device(n + 1))
            )
            copies[-1].start()
        for copy in copies:
            copy.wait()
        for n in range(3):
            squares = squares + norm_recv[n]
        for b in range(2):
            norm = jnp.sqrt(jnp.sum(squares[b], axis=(0, 1), keepdims=True))
            radius = radii_ref[0, b]
            dual_out[b] = error[b] - error[b] * (radius / jnp.maximum(norm, radius))

    def sum_start(step, value, devices):
        sums[step] = value
        copies = []
        for n, device in enumerate(devices):
            copies.append(
                remote(sums.at[step], parts.at[step, n], small_sends.at[step, n], small_recvs.at[step, n], device)
            )
            copies[-1].start()
        return copies

    def sum_end(step, copies):
        for copy in copies:
            copy.wait()
        value = sums[step]
        for n in range(len(copies)):
            value = value + parts[step, n]
        return value

    group_a = [{"chan": chan_peer(offset)} for offset in GROUP_A]
    group_b = [group_b_device(offset) for offset in GROUP_B]

    gathers = gather_start(dual_ref, 0)
    duals[0, place] = dual_ref[...]
    for b in range(2):
        rad[vis, b] = jnp.full((8, 128), radii_ref[0, b], jnp.float32)
    rad_copy = remote(rad.at[vis], rad.at[vis], rad_sems.at[0], rad_sems.at[1], {"vis": 1 - vis})
    rad_copy.start()
    for copy in loads[:2]:
        copy.wait()

    def subtract(k, carry):
        rows = pl.ds(pl.multiple_of(k * 64, 64), 64)
        change[rows, :] = p_now[rows, :] - x_now[rows, :]
        return carry

    lax.fori_loop(0, ROWS // 64, subtract, 0)
    first = send_tiles(0, change, got_change, OFFSETS + [(0, 0, 0)])
    for copy in loads[2:]:
        copy.wait()
    build_tables(tiles_ref, wave_q, wave_p, waves_q, waves_p, lanes, subs, tabs)
    for copy in gathers:
        copy.wait()
    spread_rows(duals.at[0], None, rowt_h, rowt_l, e_h, e_l)

    for d in (2, 1, 3, 0):
        chunk = column_chunk(d)
        cols = chunk_columns(chunk)
        x = x_now[:, cols]
        x_new = jnp.maximum(0.0, x - step_size * (p_now[:, cols] + adjoint_chunk(chunk)))
        put(x_h, x_l, (slice(None), cols), 2.0 * x_new - x)
        x_now[:, cols] = x_new
    first += send_tiles(1, x_now, got_x, OFFSETS + [(0, 0, 0)])

    error_mid[...] = residual(0, scatter_start(0), dual_ref[...])
    gathers = gather_start(error_mid, 1)
    duals[1, place] = error_mid[...]
    rad_copy.wait()
    for copy in first:
        copy.wait()
    total = pack(gram_of(lambda rows: got_change[rows, :] + 2.0 * got_x[rows, :], halves))
    small = sum_start(0, total, group_a)
    for copy in gathers:
        copy.wait()
    spread_rows(duals.at[1], gain_of, rowt_h, rowt_l, e_h, e_l)
    small = sum_start(1, sum_end(0, small), group_b)
    second = []
    for d in (2, 1, 3, 0):
        chunk = column_chunk(d)
        slope[:, chunk_columns(chunk)] = adjoint_chunk(chunk)
        second += send_tiles(2, slope, got_slope, chunk_offsets(d))
    total = sum_end(1, small)
    mix_into(mixed.at[0], halves, inverse_root(unpack(total), radius_ref[0]))
    third = send_back(3, p_back.at[me], OFFSETS[:8])
    p_back[me] = mixed[0, lane_rows(me), :]
    for copy in second:
        copy.wait()
    total = gram_of(
        lambda rows: jnp.maximum(mixed[0, rows, :] - got_x[rows, :], got_x[rows, :] - got_slope[rows, :]), halves
    )
    small = sum_start(2, pack(total), group_a)
    third += send_back(3, p_back.at[me], OFFSETS[8:14])
    small = sum_start(3, sum_end(2, small), group_b)
    third += send_back(3, p_back.at[me], OFFSETS[14:20])
    total = sum_end(3, small)
    third += send_back(3, p_back.at[me], OFFSETS[20:])
    mix_into(mixed.at[1], halves, inverse_root(unpack(total), radius_ref[0]))
    rows, cols = tile_place(me)
    p_store = pltpu.make_async_copy(mixed.at[1, lane_rows(me), :], p_out.at[rows, cols], local_sems.at[7])
    p_store.start()
    fourth = send_back(4, p_out.at[rows, cols], OFFSETS)

    for n, offset in enumerate(OFFSETS + [(0, 0, 0)]):
        j = chan_peer(negated(offset))
        if n < len(OFFSETS):
            third[n].wait_recv()
        rows, cols = tile_place(j)
        x = x_now[rows, cols]
        x_new = jnp.maximum(0.0, x - step_size * (p_back[j] + slope[rows, cols]))
        put(x_h, x_l, (rows, cols), 2.0 * x_new - x)
        x_now[rows, cols] = x_new
    x_store = pltpu.make_async_copy(x_now, x_out, local_sems.at[6])
    x_store.start()
    last_dual(scatter_start(1))
    for copy in third:
        copy.wait_send()
    x_store.wait()
    p_store.wait()
    for copy in fourth:
        copy.wait()


def store_kernel(x_in, p_in, dual_in, x_out, p_out, dual_out, x_buf, p_buf, dual_buf, load_sems, store_sems):
    moves = []
    for source, buffer, target in ((x_in, x_buf, x_out), (p_in, p_buf, p_out)):
        for k in range(4):
            rows = slice(k * 128, (k + 1) * 128)
            moves.append((source.at[rows], buffer.at[rows], target.at[0, rows]))
    moves.append((dual_in, dual_buf, dual_out.at[0]))
    loads = [pltpu.make_async_copy(a, b, load_sems.at[n]) for n, (a, b, c) in enumerate(moves)]
    stores = [pltpu.make_async_copy(b, c, store_sems.at[n]) for n, (a, b, c) in enumerate(moves)]
    for copy in loads:
        copy.start()
    for load, store in zip(loads, stores):
        load.wait()
        store.start()
    for copy in stores:
        copy.wait()


def on_device(cube, lowrank_dual, vis_dual, visibilities, radii, tiles, facet_radius):
    f32, bf16 = jnp.float32, jnp.bfloat16
    dma = pltpu.SemaphoreType.DMA
    vmem = pl.BlockSpec(memory_space=pltpu.VMEM)
    smem = pl.BlockSpec(memory_space=pltpu.SMEM)
    anywhere = pl.BlockSpec(memory_space=pl.ANY)
    own = vis_dual.shape[1:]
    image = (ROWS, COLS)
    cube_next, lowrank_next, vis_next = pl.pallas_call(
        imaging_kernel,
        out_shape=[
            jax.ShapeDtypeStruct(image, f32),
            jax.ShapeDtypeStruct(image, f32),
            jax.ShapeDtypeStruct(own, f32),
        ],
        in_specs=[anywhere, anywhere, vmem, vmem, smem, smem, smem, anywhere, anywhere, vmem, vmem],
        out_specs=[anywhere, anywhere, vmem],
        scratch_shapes=[
            pltpu.VMEM(image, f32),
            pltpu.VMEM(image, f32),
            pltpu.VMEM(image, f32),
            pltpu.VMEM(image, f32),
            pltpu.VMEM((CHANNELS, TILE, TILE), f32),
            pltpu.VMEM((CHANNELS * PITCH, TILE), f32),
            pltpu.VMEM((CHANNELS * PITCH, TILE), f32),
            pltpu.VMEM((CHANNELS * PITCH, TILE), f32),
            pltpu.VMEM((2, CHANNELS * PITCH, TILE), f32),
            pltpu.VMEM((TILE // 8, 2 * CHANNELS, 1024), bf16),
            pltpu.VMEM(image, bf16),
            pltpu.VMEM(image, bf16),
            pltpu.VMEM(image, bf16),
            pltpu.VMEM(image, bf16),
            pltpu.VMEM((COLS // CHUNK, BLOCKS * 256, CHUNK), bf16),
            pltpu.VMEM((COLS // CHUNK, BLOCKS * 256, CHUNK), bf16),
            pltpu.VMEM((BLOCKS, COLS, 256), bf16),
            pltpu.VMEM((BLOCKS, COLS, 256), bf16),
            pltpu.VMEM((BLOCKS, 256, ROWS), bf16),
            pltpu.VMEM((BLOCKS, 256, ROWS), bf16),
            pltpu.VMEM((BLOCKS, ROWS, 256), bf16),
            pltpu.VMEM((BLOCKS, ROWS, 256), bf16),
            pltpu.VMEM((2, TILE, COLS), f32),
            pltpu.VMEM((2, TILE, ROWS), f32),
            pltpu.VMEM((2, COLS, TILE), f32),
            pltpu.VMEM((2, ROWS, TILE), f32),
            pltpu.VMEM((2, 8) + own, f32),
            pltpu.VMEM(own, f32),
            pltpu.VMEM((BLOCKS, 2, TILE, TILE), f32),
            pltpu.VMEM((2, 7) + own, f32),
            pltpu.VMEM((2, 2, 8, 128), f32),
            pltpu.VMEM((2, 2, 8, 128), f32),
            pltpu.VMEM((2, 8, 128), f32),
            pltpu.VMEM((3, 2, 8, 128), f32),
            pltpu.VMEM((4, 8, 128), f32),
            pltpu.VMEM((4, 7, 8, 128), f32),
            dma((8,)),
            dma((5, 31)),
            dma((5, 31)),
            dma((2, 7)),
            dma((2, 7)),
            dma((2, 7, 2)),
            dma((2, 7, 2)),
            dma((2,)),
            dma((3,)),
            dma((3,)),
            dma((4, 7)),
            dma((4, 7)),
        ],
        compiler_params=pltpu.CompilerParams(
            collective_id=0, has_side_effects=True, vmem_limit_bytes=56 << 20
        ),
        name="imaging",
    )(
        cube[0], lowrank_dual[0], vis_dual[0], visibilities[0], radii, jnp.swapaxes(tiles, 1, 2), facet_radius,
        *[jnp.asarray(value) for value in waves()],
    )
    return pl.pallas_call(
        store_kernel,
        out_shape=[
            jax.ShapeDtypeStruct((1,) + image, f32),
            jax.ShapeDtypeStruct((1,) + image, f32),
            jax.ShapeDtypeStruct((1,) + own, f32),
        ],
        in_specs=[anywhere] * 3,
        out_specs=[anywhere] * 3,
        scratch_shapes=[pltpu.VMEM(image, f32), pltpu.VMEM(image, f32), pltpu.VMEM(own, f32), dma((9,)), dma((9,))],
        compiler_params=pltpu.CompilerParams(vmem_limit_bytes=56 << 20),
        name="store",
    )(cube_next, lowrank_next, vis_next)


def solution(mesh):
    placed = (
        P("chan", "facet", "vis"),
        P("chan", "facet", "vis"),
        P("chan", "vis", None, "facet", None),
        P("chan", "vis", None, "facet", None),
        P("chan", "vis"),
        P("chan", None, None),
        P("facet"),
    )
    return jax.shard_map(
        on_device,
        mesh=mesh,
        in_specs=placed,
        out_specs=(
            P("chan", "facet", "vis"),
            P("chan", "facet", "vis"),
            P("chan", "vis", None, "facet", None),
        ),
        check_vma=False,
    )
```
